512 devices in a mesh: loop: 256 (over x_lo, y, z, core), query: 2 (over x_hi).
Axes of the slice: x: 4 (x_hi: 2, x_lo: 2; x = x_hi * 2 + x_lo), y: 4, z: 16, core: 2. Of those that a mesh axis runs over, the one named last changes fastest.
Arguments:
- coefficients: bfloat16 [32, 3, 128], P('query'), may hold values from -0.3125 to 0.3125
- mode_basis: bfloat16 [3, 128, 8192, 128], P(None, None, 'loop'), may hold values from -6 to 6
- shifts: int32 [32, 3], replicated, may hold values from 0 to 8191
- owners: int32 [32], replicated, may hold values from 0 to 1, as said below
Outputs:
- reconstruction: float32 [32, 8192, 128], P('query', 'loop')
- sensor: float32 [32, 8192, 128], P('query', 'loop')
The draws below stay inside these ranges and needn't reach their ends.
Inputs may be any that keep to these rules, and one draw needn't show every extreme that they name: Each of the 2 owners owns exactly 16 queries.
All inputs are finite; a program needn't handle non-finite values.
Results may differ from the reference program's by a relative error of at most 0.0032.
Values may be sent and summed in bfloat16 or wider, within the bound.
A program may use at most 64 MiB of HBM per device.

```python
import jax
import jax.numpy as jnp

M = 128
NC = 128
F = 3
Q = 32
QDEV = 16
NS = 8192


def draw_owners(key, part):
    key = jax.random.fold_in(key, 7)
    shuffled = jax.random.permutation(key, Q)
    return (shuffled // QDEV).astype(jnp.int32)


def with_ends(array, rng, smallest, high):
    place = [jax.random.randint(jax.random.fold_in(rng, axis), (), 0, length) for axis, length in enumerate(array.shape)]
    longest = array.shape.index(max(array.shape))
    beside = place[:longest] + [(place[longest] + 1) % array.shape[longest]] + place[longest + 1:]
    return array.at[tuple(place)].set(smallest).at[tuple(beside)].set(high)


def levels(own_key, shape, split, low, largest):
    def one(axis_at, shards_of):
        heights = jax.random.uniform(jax.random.fold_in(jax.random.fold_in(own_key, 6), axis_at), (shards_of,), jnp.float32, low / len(split), largest / len(split))
        return jnp.repeat(jnp.exp(heights), shape[axis_at] // shards_of).reshape((-1,) + (1,) * (len(shape) - axis_at - 1))

    loudness = one(*split[0])
    for cut in split[1:]:
        loudness = loudness * one(*cut)
    return loudness


def noise(own_key, shape, scale, most, shards=(), kind=jnp.bfloat16):
    array = jax.random.normal(own_key, shape, jnp.float32) * scale
    if len(shards) > 0:
        array = levels(own_key, shape, shards, -0.22, 0.18) * array
    return jnp.clip(array, min=-most, max=most).astype(kind)


def setup_inputs(seed: int = 0) -> dict:
    streams_of = jax.random.split(jax.random.key(seed), 5)
    coefficients = noise(streams_of[0], (Q, F, M), (3 * M) ** -0.5, 0.3125, ((0, 2),))
    mode_basis = noise(streams_of[1], (F, M, NS, NC), 1.0, 6.0, ((2, 256),))
    shifts = with_ends(jax.random.randint(streams_of[2], (Q, F), 0, NS), jax.random.fold_in(streams_of[2], 1), 0, NS - 1).astype(jnp.int32)
    owners = draw_owners(jax.random.fold_in(streams_of[4], 71), 0)
    return dict(coefficients=coefficients, mode_basis=mode_basis, shifts=shifts, owners=owners)


def reference(coefficients, mode_basis, shifts, owners):
    order = jnp.argsort(owners, stable=True).astype(jnp.int32)
    chosen = coefficients[order]
    chosen_shifts = shifts[order]
    positions = jnp.arange(NS, dtype=jnp.int32)
    total = jnp.zeros((Q, NS, NC), jnp.float32)
    for frame in range(F):
        fields = jnp.dot(chosen[:, frame, :], mode_basis[frame].reshape(M, NS * NC), preferred_element_type=jnp.float32)
        fields = fields.astype(jnp.bfloat16).reshape(Q, NS, NC)
        sources = (positions[None, :] - chosen_shifts[:, frame][:, None]) % NS
        moved = jax.vmap(lambda block, rows: block[rows])(fields, sources.astype(jnp.int32))
        total = total + moved.astype(jnp.float32)
    center = total
    upper = jnp.roll(total, -1, axis=1)
    lower = jnp.roll(total, 1, axis=1)
    padded = jnp.pad(total, ((0, 0), (0, 0), (1, 1)))
    right_side = padded[:, :, 2:]
    left_side = padded[:, :, :-2]
    numerator = jnp.abs(upper - 2.0 * center + lower) + jnp.abs(right_side - 2.0 * center + left_side)
    denominator = jnp.maximum(jnp.abs(upper) + 2.0 * jnp.abs(center) + jnp.abs(lower), 1.0)
    return total, numerator / denominator
```

```python
import functools

import jax
import jax.numpy as jnp
from jax import lax
from jax.experimental import pallas as pl
from jax.experimental.pallas import tpu as pltpu
from jax.sharding import PartitionSpec as P

MESH = pl.DeviceIdType.MESH
RING = 16
LANES = 128
WIDE = 8


def swapped(tiles):
    lane = lax.broadcasted_iota(jnp.int32, tiles[0].shape, 1)
    for bit in range(4):
        step = 1 << bit
        width = step * WIDE
        low = (lane // width) % 2 == 0
        new = [None] * RING
        for i in range(RING):
            if i & step:
                continue
            a, b = tiles[i], tiles[i | step]
            new[i] = jnp.where(low, a, pltpu.roll(b, width, 1))
            new[i | step] = jnp.where(low, pltpu.roll(a, LANES - width, 1), b)
        tiles = new
    return tiles


def kernel(
    coef, pick_own, pick_other, basis, shift, recon, sensor,
    coef_in, raw, modes, s1, r1, s2, r2, long, s3, r3, s4, r4, field,
    basis_sem, coef_send, coef_recv, send1, recv1, own1, send2, recv2, own2,
    send3, recv3, own3, send4, recv4, own4, halo_send, halo_recv,
):
    me = lax.axis_index("loop")
    group = lax.axis_index("query")
    devices = lax.axis_size("loop")
    core = me % 2
    z = (me // 2) % RING
    sup = me // (2 * RING)
    spot = sup * 2 + core
    before = (me + devices - 1) % devices
    after = (me + 1) % devices

    def at_z(i):
        return sup * (2 * RING) + i * 2 + core

    def at_spot(i):
        return (i // 2) * (2 * RING) + z * 2 + i % 2

    frames = basis.shape[0]
    loads = [pltpu.make_async_copy(basis.at[f], raw.at[f], basis_sem.at[f]) for f in range(frames)]
    for load in loads:
        load.start()

    barrier = pltpu.get_barrier_semaphore()

    def greet(d, carry):
        pl.semaphore_signal(barrier, inc=1, device_id={"loop": at_z((z + d) % RING)}, device_id_type=MESH)
        pl.semaphore_signal(barrier, inc=1, device_id={"loop": at_spot((spot + d) % RING)}, device_id_type=MESH)
        return carry

    pl.semaphore_signal(barrier, inc=1, device_id={"query": 1 - group}, device_id_type=MESH)
    pl.semaphore_signal(barrier, inc=1, device_id={"loop": before}, device_id_type=MESH)
    pl.semaphore_signal(barrier, inc=1, device_id={"loop": after}, device_id_type=MESH)
    lax.fori_loop(1, RING, greet, 0)
    pl.semaphore_wait(barrier, 2 * (RING - 1) + 3)

    exchange = pltpu.make_async_remote_copy(
        src_ref=coef, dst_ref=coef_in, send_sem=coef_send, recv_sem=coef_recv,
        device_id={"query": 1 - group}, device_id_type=MESH,
    )
    exchange.start()

    def spread(source, target, here, to, send_sem, recv_sem, own_sem):
        pltpu.make_async_copy(source.at[here], target.at[here], own_sem).start()

        def one(d, carry):
            i = (here + d) % RING
            pltpu.make_async_remote_copy(
                src_ref=source.at[i], dst_ref=target.at[here], send_sem=send_sem, recv_sem=recv_sem,
                device_id={"loop": to(i)}, device_id_type=MESH,
            ).start()
            return carry

        lax.fori_loop(1, RING, one, 0)

    def landed(source, target, here, recv_sem, own_sem):
        pltpu.make_async_copy(source.at[here], target.at[here], own_sem).wait()
        most = target.at[pl.ds(0, RING - 1)]
        pltpu.make_async_copy(most, most, recv_sem).wait()

    def sent(source, send_sem):
        most = source.at[pl.ds(0, RING - 1)]
        pltpu.make_async_copy(most, most, send_sem).wait()

    for f in range(frames):
        loads[f].wait()
        modes[f] = jnp.swapaxes(raw[f], 0, 1)
    exchange.wait()
    chosen = jnp.dot(pick_own[...], coef[...], preferred_element_type=jnp.float32)
    chosen = chosen + jnp.dot(pick_other[...], coef_in[...], preferred_element_type=jnp.float32)
    chosen = chosen.astype(jnp.bfloat16)

    for f in range(frames):
        weights = chosen[:, f * LANES:(f + 1) * LANES]
        for half in range(2):
            tiles = [
                jnp.dot(weights, modes[f, half * RING + x], preferred_element_type=jnp.float32).astype(jnp.bfloat16)
                for x in range(RING)
            ]
            tiles = swapped(tiles)
            for i in range(RING):
                s1[f, i, half] = tiles[i]
        spread(s1.at[f], r1.at[f], z, at_z, send1.at[f], recv1.at[f], own1.at[f])

    for f in range(frames):
        landed(s1.at[f], r1.at[f], z, recv1.at[f], own1.at[f])
        for half in range(2):
            s2[f, :, half] = jnp.swapaxes(r1[f, :, half], 0, 1)
        spread(s2.at[f], r2.at[f], spot, at_spot, send2.at[f], recv2.at[f], own2.at[f])

    for f in range(frames):
        landed(s2.at[f], r2.at[f], spot, recv2.at[f], own2.at[f])
        for c in range(2):
            for half in range(2):
                for i in range(8):
                    part = r2[f, i * 2 + c, half].astype(jnp.float32)
                    long[f, c * 2 + half, i * 16:(i + 1) * 16] = part
                    long[f, c * 2 + half, 128 + i * 16:128 + (i + 1) * 16] = part

    lane = lax.broadcasted_iota(jnp.int32, (128, LANES), 1)
    for j in range(4):
        total = None
        for f in range(frames):
            cells = shift[f]
            rows = cells // 16
            turn = (cells % 16) * WIDE

            def moved(rows):
                low = rows % 4
                down = (rows // 4 + (j < low).astype(jnp.int32)) % 128
                return long[f, (j + 4 - low) % 4, pl.ds(128 - down, 128), :]

            both = jnp.where(lane >= LANES - turn, moved(rows + 1), moved(rows))
            both = pltpu.roll(both, turn, 1)
            total = both if total is None else total + both
        total = total.astype(jnp.bfloat16)
        for i in range(8):
            s3[i * 2 + j // 2, j % 2] = total[i * 16:(i + 1) * 16]

    spread(s3, r3, spot, at_spot, send3, recv3, own3)
    landed(s3, r3, spot, recv3, own3)
    for half in range(2):
        s4[:, half] = jnp.swapaxes(r3[:, half], 0, 1)
    spread(s4, r4, z, at_z, send4, recv4, own4)
    landed(s4, r4, z, recv4, own4)
    for half in range(2):
        tiles = swapped([r4[i, half] for i in range(RING)])
        for i in range(RING):
            field[1 + half * RING + i] = tiles[i]

    length = 2 * RING
    up = pltpu.make_async_remote_copy(
        src_ref=field.at[length], dst_ref=field.at[0], send_sem=halo_send.at[0], recv_sem=halo_recv.at[0],
        device_id={"loop": after}, device_id_type=MESH,
    )
    down = pltpu.make_async_remote_copy(
        src_ref=field.at[1], dst_ref=field.at[length + 1], send_sem=halo_send.at[1], recv_sem=halo_recv.at[1],
        device_id={"loop": before}, device_id_type=MESH,
    )
    up.start()
    down.start()
    recon[...] = jnp.swapaxes(field[1:length + 1].astype(jnp.float32), 0, 1)

    place = lax.broadcasted_iota(jnp.int32, (RING, LANES), 1)

    def sense(x):
        lower = field[x].astype(jnp.float32)
        center = field[x + 1].astype(jnp.float32)
        upper = field[x + 2].astype(jnp.float32)
        right = jnp.where(place == LANES - 1, 0.0, pltpu.roll(center, LANES - 1, 1))
        left = jnp.where(place == 0, 0.0, pltpu.roll(center, 1, 1))
        numerator = jnp.abs(upper - 2.0 * center + lower) + jnp.abs(right - 2.0 * center + left)
        denominator = jnp.maximum(jnp.abs(upper) + 2.0 * jnp.abs(center) + jnp.abs(lower), 1.0)
        return numerator / denominator

    inner = {x: sense(x) for x in range(1, length - 1)}
    up.wait()
    down.wait()
    inner[0] = sense(0)
    inner[length - 1] = sense(length - 1)
    sensor[...] = jnp.swapaxes(jnp.stack([inner[x] for x in range(length)]), 0, 1)

    for f in range(frames):
        sent(s1.at[f], send1.at[f])
        sent(s2.at[f], send2.at[f])
    sent(s3, send3)
    sent(s4, send4)


def shards(coefficients, mode_basis, shifts, owners):
    per_device = coefficients.shape[0]
    frames, modes, rows, cells = mode_basis.shape
    group = lax.axis_index("query")
    me = lax.axis_index("loop")
    spot = (me // (2 * RING)) * 2 + me % 2
    mine = owners == group
    index = jnp.arange(owners.shape[0], dtype=jnp.int32)
    rank = jnp.sum((mine[None, :] & (index[None, :] < index[:, None])).astype(jnp.int32), axis=1)
    slots = jnp.arange(per_device, dtype=jnp.int32)
    picked = mine[None, :] & (rank[None, :] == slots[:, None])
    shift = jnp.sum(jnp.where((mine & (rank == spot))[:, None], shifts, 0), axis=0)
    picked = picked.astype(jnp.bfloat16)
    first, second = picked[:, :per_device], picked[:, per_device:]
    pick_own = jnp.where(group == 0, first, second)
    pick_other = jnp.where(group == 0, second, first)
    bf16, f32 = jnp.bfloat16, jnp.float32
    block = (RING, 2, RING, LANES)
    vmem = pl.BlockSpec(memory_space=pltpu.VMEM)
    dma = pltpu.SemaphoreType.DMA
    recon, sensor = pl.pallas_call(
        kernel,
        out_shape=[jax.ShapeDtypeStruct((per_device, rows, cells), f32)] * 2,
        in_specs=[vmem, vmem, vmem, pl.BlockSpec(memory_space=pl.ANY), pl.BlockSpec(memory_space=pltpu.SMEM)],
        out_specs=[vmem, vmem],
        scratch_shapes=[
            pltpu.VMEM((per_device, frames * modes), bf16),
            pltpu.VMEM((frames, modes, rows, cells), bf16),
            pltpu.VMEM((frames, rows, modes, cells), bf16),
            pltpu.VMEM((frames,) + block, bf16),
            pltpu.VMEM((frames,) + block, bf16),
            pltpu.VMEM((frames,) + block, bf16),
            pltpu.VMEM((frames,) + block, bf16),
            pltpu.VMEM((frames, 4, 256, LANES), f32),
            pltpu.VMEM(block, bf16),
            pltpu.VMEM(block, bf16),
            pltpu.VMEM(block, bf16),
            pltpu.VMEM(block, bf16),
            pltpu.VMEM((rows + 2, per_device, cells), bf16),
            dma((frames,)), dma(()), dma(()),
            dma((frames,)), dma((frames,)), dma((frames,)),
            dma((frames,)), dma((frames,)), dma((frames,)),
            dma(()), dma(()), dma(()),
            dma(()), dma(()), dma(()),
            dma((2,)), dma((2,)),
        ],
        compiler_params=pltpu.CompilerParams(
            collective_id=0, has_side_effects=True, vmem_limit_bytes=40 * 1024 * 1024
        ),
    )(coefficients.reshape(per_device, frames * modes), pick_own, pick_other, mode_basis, shift)
    return recon, sensor


def solution(mesh):
    placed = (P("query", None, None), P(None, None, "loop", None), P(), P())
    return jax.shard_map(
        shards,
        mesh=mesh,
        in_specs=placed,
        out_specs=(P("query", "loop", None), P("query", "loop", None)),
        check_vma=False,
    )
```

```python
import functools

import jax
import jax.numpy as jnp
from jax import lax
from jax.experimental import pallas as pl
from jax.experimental.pallas import tpu as pltpu
from jax.sharding import PartitionSpec as P

MESH = pl.DeviceIdType.MESH
RING = 16
LANES = 128
WIDE = 4
PARTS = 2


def swapped(tiles):
    lane = lax.broadcasted_iota(jnp.int32, tiles[0].shape, 1)
    count = len(tiles)
    step = 1
    while step < count:
        width = step * (LANES // count)
        low = (lane // width) % 2 == 0
        new = [None] * count
        for i in range(count):
            if i & step:
                continue
            a, b = tiles[i], tiles[i | step]
            new[i] = jnp.where(low, a, pltpu.roll(b, width, 1))
            new[i | step] = jnp.where(low, pltpu.roll(a, LANES - width, 1), b)
        tiles = new
        step = step * 2
    return tiles


def kernel(
    coef, basis, shifts, owners, field,
    shift_in, owner_in, owner_row, coefs, raw, modes, s1, r1, s2, r2, long, s3, r3, s4, r4,
    basis_sem, small_sem, coef_send, coef_recv, send1, recv1, own1, send2, recv2, own2,
    send3, recv3, own3, send4, recv4, own4, halo_send, halo_recv,
):
    me = lax.axis_index("loop")
    group = lax.axis_index("query")
    devices = lax.axis_size("loop")
    core = me % 2
    z = (me // 2) % RING
    sup = me // (2 * RING)
    spot = sup * 2 + core
    before = (me + devices - 1) % devices
    after = (me + 1) % devices

    def at_z(i):
        return sup * (2 * RING) + i * 2 + core

    def at_spot(i):
        return (i // 2) * (2 * RING) + z * 2 + i % 2

    barrier = pltpu.get_barrier_semaphore()

    def greet_z(k, carry):
        d = RING // 2 + (1 - 2 * (k % 2)) * ((k + 1) // 2)
        pl.semaphore_signal(barrier, inc=1, device_id={"loop": at_z((z + d) % RING)}, device_id_type=MESH)
        return carry

    def greet(d, carry):
        pl.semaphore_signal(barrier, inc=1, device_id={"loop": at_spot((spot + d) % RING)}, device_id_type=MESH)
        return carry

    lax.fori_loop(0, RING - 1, greet_z, 0)
    pl.semaphore_signal(barrier, inc=1, device_id={"query": 1 - group}, device_id_type=MESH)
    lax.fori_loop(1, RING, greet, 0)
    pl.semaphore_signal(barrier, inc=1, device_id={"loop": before}, device_id_type=MESH)
    pl.semaphore_signal(barrier, inc=1, device_id={"loop": after}, device_id_type=MESH)

    frames = basis.shape[0]
    mine_at = pl.ds(pl.multiple_of(group * RING, RING), RING)
    small = [
        pltpu.make_async_copy(owners, owner_row, small_sem.at[0]),
        pltpu.make_async_copy(coef, coefs.at[:, mine_at], small_sem.at[1]),
        pltpu.make_async_copy(owners, owner_in, small_sem.at[2]),
        pltpu.make_async_copy(shifts, shift_in, small_sem.at[3]),
    ]
    loads = [pltpu.make_async_copy(basis.at[f], raw.at[f], basis_sem.at[f]) for f in range(frames)]
    for load in small + loads:
        load.start()
    pl.semaphore_wait(barrier, 2 * (RING - 1) + 3)
    exchange = pltpu.make_async_remote_copy(
        src_ref=coef, dst_ref=coefs.at[:, mine_at], send_sem=coef_send, recv_sem=coef_recv,
        device_id={"query": 1 - group}, device_id_type=MESH,
    )
    exchange.start()

    def spread(source, target, here, to, send_sem, recv_sem, own_sem):
        pltpu.make_async_copy(source.at[here], target.at[here], own_sem).start()

        def one(d, carry):
            i = (here + d) % RING
            pltpu.make_async_remote_copy(
                src_ref=source.at[i], dst_ref=target.at[here], send_sem=send_sem, recv_sem=recv_sem,
                device_id={"loop": to(i)}, device_id_type=MESH,
            ).start()
            return carry

        lax.fori_loop(1, RING, one, 0)

    def landed(source, target, here, recv_sem, own_sem):
        pltpu.make_async_copy(source.at[here], target.at[here], own_sem).wait()
        most = target.at[pl.ds(0, RING - 1)]
        pltpu.make_async_copy(most, most, recv_sem).wait()

    def sent(source, send_sem):
        most = source.at[pl.ds(0, RING - 1)]
        pltpu.make_async_copy(most, most, send_sem).wait()

    queries = owners.shape[1]
    small[0].wait()
    mine = (owner_row[...] == group).astype(jnp.float32)
    mine = jnp.broadcast_to(mine, (RING, queries))
    row = lax.broadcasted_iota(jnp.int32, (queries, queries), 0)
    column = lax.broadcasted_iota(jnp.int32, (queries, queries), 1)
    triangle = (row < column).astype(jnp.bfloat16)
    rank = jnp.dot(mine.astype(jnp.bfloat16), triangle, preferred_element_type=jnp.float32)
    slot = lax.broadcasted_iota(jnp.int32, (RING, queries), 0).astype(jnp.float32)
    picked = jnp.where(rank == slot, mine, 0.0).astype(jnp.bfloat16)
    small[1].wait()

    def first(h, f):
        spread(s1.at[h, f], r1.at[h, f], z, at_z, send1.at[h, f], recv1.at[h, f], own1.at[h, f])

    for f in range(frames):
        loads[f].wait()
        modes[f] = jnp.swapaxes(raw[f], 0, 1)
        if f == 0:
            exchange.wait()
        weights = jnp.dot(picked, coefs[f], preferred_element_type=jnp.float32).astype(jnp.bfloat16)
        tiles = [
            jnp.dot(weights, modes[f, x], preferred_element_type=jnp.float32).astype(jnp.bfloat16)
            for x in range(2 * RING)
        ]
        tiles = swapped(tiles)
        for h in range(PARTS):
            for i in range(RING):
                s1[h, f, i] = tiles[h * RING + i]
        first(0, f)
    for f in range(frames):
        first(1, f)

    small[2].wait()
    small[3].wait()
    count = jnp.int32(0)
    cells_of = [jnp.int32(0)] * frames
    for q in range(queries):
        own = owner_in[0, q] == group
        here = jnp.logical_and(own, count == spot)
        cells_of = [jnp.where(here, shift_in[f, q], cells_of[f]) for f in range(frames)]
        count = count + own.astype(jnp.int32)

    def second(h):
        for f in range(frames):
            landed(s1.at[h, f], r1.at[h, f], z, recv1.at[h, f], own1.at[h, f])
            s2[h, f] = jnp.swapaxes(r1[h, f], 0, 1)
            spread(s2.at[h, f], r2.at[h, f], spot, at_spot, send2.at[h, f], recv2.at[h, f], own2.at[h, f])

    lane = lax.broadcasted_iota(jnp.int32, (128, LANES), 1)

    def third(h):
        for f in range(frames):
            landed(s2.at[h, f], r2.at[h, f], spot, recv2.at[h, f], own2.at[h, f])
            for i in range(RING):
                part = r2[h, f, i].astype(jnp.float32)
                at = (i // 2) * RING
                long[h, f, i % 2, at:at + RING] = part
                long[h, f, i % 2, 128 + at:128 + at + RING] = part
        for j in range(2):
            total = None
            for f in range(frames):
                rows = cells_of[f] // 32
                turn = (cells_of[f] % 32) * WIDE

                def moved(rows):
                    low = rows % 2
                    down = (rows // 2 + (j < low).astype(jnp.int32)) % 128
                    return long[h, f, (j + 2 - low) % 2, pl.ds(128 - down, 128), :]

                both = jnp.where(lane >= LANES - turn, moved(rows + 1), moved(rows))
                both = pltpu.roll(both, turn, 1)
                total = both if total is None else total + both
            total = total.astype(jnp.bfloat16)
            for i in range(8):
                s3[h, i * 2 + j] = total[i * RING:(i + 1) * RING]
        spread(s3.at[h], r3.at[h], spot, at_spot, send3.at[h], recv3.at[h], own3.at[h])

    def fourth(h):
        landed(s3.at[h], r3.at[h], spot, recv3.at[h], own3.at[h])
        s4[h] = jnp.swapaxes(r3[h], 0, 1)
        spread(s4.at[h], r4.at[h], z, at_z, send4.at[h], recv4.at[h], own4.at[h])

    second(0)
    third(0)
    second(1)
    fourth(0)
    third(1)
    fourth(1)
    for h in range(PARTS):
        landed(s4.at[h], r4.at[h], z, recv4.at[h], own4.at[h])
    tiles = swapped([r4[h, i] for h in range(PARTS) for i in range(RING)])
    for x in range(2 * RING):
        field[1 + x] = tiles[x]

    length = 2 * RING
    up = pltpu.make_async_remote_copy(
        src_ref=field.at[length], dst_ref=field.at[0], send_sem=halo_send.at[0], recv_sem=halo_recv.at[0],
        device_id={"loop": after}, device_id_type=MESH,
    )
    down = pltpu.make_async_remote_copy(
        src_ref=field.at[1], dst_ref=field.at[length + 1], send_sem=halo_send.at[1], recv_sem=halo_recv.at[1],
        device_id={"loop": before}, device_id_type=MESH,
    )
    up.start()
    down.start()
    for h in range(PARTS):
        for f in range(frames):
            sent(s1.at[h, f], send1.at[h, f])
            sent(s2.at[h, f], send2.at[h, f])
        sent(s3.at[h], send3.at[h])
        sent(s4.at[h], send4.at[h])
    up.wait()
    down.wait()


def finish(field, recon, sensor):
    u = field[...].astype(jnp.float32)
    center, upper, lower = u[1:-1], u[2:], u[:-2]
    recon[...] = jnp.swapaxes(center, 0, 1)
    place = lax.broadcasted_iota(jnp.int32, center.shape, 2)
    right = jnp.where(place == LANES - 1, 0.0, pltpu.roll(center, LANES - 1, 2))
    left = jnp.where(place == 0, 0.0, pltpu.roll(center, 1, 2))
    numerator = jnp.abs(upper - 2.0 * center + lower) + jnp.abs(right - 2.0 * center + left)
    denominator = jnp.maximum(jnp.abs(upper) + 2.0 * jnp.abs(center) + jnp.abs(lower), 1.0)
    sensor[...] = jnp.swapaxes(numerator / denominator, 0, 1)


def shards(coefficients, mode_basis, shifts, owners):
    per_device = coefficients.shape[0]
    queries = owners.shape[0]
    frames, modes, rows, cells = mode_basis.shape
    bf16, f32 = jnp.bfloat16, jnp.float32
    block = (RING, RING, LANES)
    hbm = pl.BlockSpec(memory_space=pltpu.HBM)
    dma = pltpu.SemaphoreType.DMA
    field = pl.pallas_call(
        kernel,
        out_shape=jax.ShapeDtypeStruct((rows + 2, per_device, cells), bf16),
        in_specs=[hbm, hbm, hbm, hbm],
        out_specs=pl.BlockSpec(memory_space=pltpu.VMEM),
        scratch_shapes=[
            pltpu.SMEM((frames, queries), jnp.int32),
            pltpu.SMEM((1, queries), jnp.int32),
            pltpu.VMEM((1, queries), jnp.int32),
            pltpu.VMEM((frames, queries, modes), bf16),
            pltpu.VMEM((frames, modes, rows, cells), bf16),
            pltpu.VMEM((frames, rows, modes, cells), bf16),
            pltpu.VMEM((PARTS, frames) + block, bf16),
            pltpu.VMEM((PARTS, frames) + block, bf16),
            pltpu.VMEM((PARTS, frames) + block, bf16),
            pltpu.VMEM((PARTS, frames) + block, bf16),
            pltpu.VMEM((PARTS, frames, 2, 256, LANES), f32),
            pltpu.VMEM((PARTS,) + block, bf16),
            pltpu.VMEM((PARTS,) + block, bf16),
            pltpu.VMEM((PARTS,) + block, bf16),
            pltpu.VMEM((PARTS,) + block, bf16),
            dma((frames,)), dma((4,)), dma(()), dma(()),
            dma((PARTS, frames)), dma((PARTS, frames)), dma((PARTS, frames)),
            dma((PARTS, frames)), dma((PARTS, frames)), dma((PARTS, frames)),
            dma((PARTS,)), dma((PARTS,)), dma((PARTS,)),
            dma((PARTS,)), dma((PARTS,)), dma((PARTS,)),
            dma((2,)), dma((2,)),
        ],
        compiler_params=pltpu.CompilerParams(
            collective_id=0, has_side_effects=True, vmem_limit_bytes=63 * 1024 * 1024
        ),
    )(jnp.swapaxes(coefficients, 0, 1), mode_basis, shifts.T, owners.reshape(1, queries))
    part = 8
    out = pl.BlockSpec((part, rows, cells), lambda i: (i, 0, 0))
    recon, sensor = pl.pallas_call(
        finish,
        grid=(per_device // part,),
        out_shape=[jax.ShapeDtypeStruct((per_device, rows, cells), f32)] * 2,
        in_specs=[pl.BlockSpec((rows + 2, part, cells), lambda i: (0, i, 0))],
        out_specs=[out, out],
        compiler_params=pltpu.CompilerParams(vmem_limit_bytes=63 * 1024 * 1024),
    )(field)
    return recon, sensor


def solution(mesh):
    placed = (P("query", None, None), P(None, None, "loop", None), P(), P())
    return jax.shard_map(
        shards,
        mesh=mesh,
        in_specs=placed,
        out_specs=(P("query", "loop", None), P("query", "loop", None)),
        check_vma=False,
    )
```

```python
import functools

import jax
import jax.numpy as jnp
from jax import lax
from jax.experimental import pallas as pl
from jax.experimental.pallas import tpu as pltpu
from jax.sharding import PartitionSpec as P

MESH = pl.DeviceIdType.MESH
RING = 16
LANES = 128
WIDE = 4
PARTS = 2


def swapped(tiles):
    lane = lax.broadcasted_iota(jnp.int32, tiles[0].shape, 1)
    count = len(tiles)
    step = 1
    while step < count:
        width = step * (LANES // count)
        low = (lane // width) % 2 == 0
        new = [None] * count
        for i in range(count):
            if i & step:
                continue
            a, b = tiles[i], tiles[i | step]
            new[i] = jnp.where(low, a, pltpu.roll(b, width, 1))
            new[i | step] = jnp.where(low, pltpu.roll(a, LANES - width, 1), b)
        tiles = new
        step = step * 2
    return tiles


def kernel(
    coef, basis, shifts, owners, field,
    shift_in, owner_row, coefs, raw, modes, s1, r1, s2, r2, long, s3, r3, s4, r4,
    basis_sem, small_sem, send1, recv1, own1, send2, recv2, own2,
    send3, recv3, own3, send4, recv4, own4, halo_send, halo_recv,
):
    me = lax.axis_index("loop")
    group = lax.axis_index("query")
    devices = lax.axis_size("loop")
    core = me % 2
    z = (me // 2) % RING
    sup = me // (2 * RING)
    spot = sup * 2 + core
    before = (me + devices - 1) % devices
    after = (me + 1) % devices

    def at_z(i):
        return sup * (2 * RING) + i * 2 + core

    def at_spot(i):
        return (i // 2) * (2 * RING) + z * 2 + i % 2

    plane = 2 * RING
    seat = group * RING + spot

    def in_plane(i):
        return {"loop": at_spot(i % RING), "query": i // RING}

    def farthest_first(k):
        return RING // 2 + (1 - 2 * (k % 2)) * ((k + 1) // 2)

    barrier = pltpu.get_barrier_semaphore()

    def greet_z(k, carry):
        i = (z + farthest_first(k)) % RING
        pl.semaphore_signal(barrier, inc=1, device_id={"loop": at_z(i)}, device_id_type=MESH)
        return carry

    def greet_plane(d, carry):
        pl.semaphore_signal(barrier, inc=1, device_id=in_plane((seat + d) % plane), device_id_type=MESH)
        return carry

    lax.fori_loop(0, RING - 1, greet_z, 0)
    lax.fori_loop(1, plane, greet_plane, 0)
    pl.semaphore_signal(barrier, inc=1, device_id={"loop": before}, device_id_type=MESH)
    pl.semaphore_signal(barrier, inc=1, device_id={"loop": after}, device_id_type=MESH)

    frames = basis.shape[0]
    small = [
        pltpu.make_async_copy(coef, coefs, small_sem.at[0]),
        pltpu.make_async_copy(owners, owner_row, small_sem.at[1]),
        pltpu.make_async_copy(shifts, shift_in, small_sem.at[2]),
    ]
    loads = [pltpu.make_async_copy(basis.at[f], raw.at[f], basis_sem.at[f]) for f in range(frames)]
    loads[0].start()
    for load in small + loads[1:]:
        load.start()

    def spread(source, target, here, to, send_sem, recv_sem, own_sem):
        pltpu.make_async_copy(source.at[here], target.at[here], own_sem).start()

        def one(k, carry):
            i = (here + farthest_first(k)) % RING
            pltpu.make_async_remote_copy(
                src_ref=source.at[i], dst_ref=target.at[here], send_sem=send_sem, recv_sem=recv_sem,
                device_id={"loop": to(i)}, device_id_type=MESH,
            ).start()
            return carry

        lax.fori_loop(0, RING - 1, one, 0)

    def landed(source, target, here, recv_sem, own_sem):
        pltpu.make_async_copy(source.at[here], target.at[here], own_sem).wait()
        most = target.at[pl.ds(0, RING - 1)]
        pltpu.make_async_copy(most, most, recv_sem).wait()

    def sent(source, send_sem):
        most = source.at[pl.ds(0, RING - 1)]
        pltpu.make_async_copy(most, most, send_sem).wait()

    def first(h, f):
        spread(s1.at[h, f], r1.at[h, f], z, at_z, send1.at[h, f], recv1.at[h, f], own1.at[h, f])

    for f in range(frames):
        loads[f].wait()
        modes[f] = jnp.swapaxes(raw[f], 0, 1)
        if f == 0:
            small[0].wait()
        weights = coefs[f]
        tiles = [
            jnp.dot(weights, modes[f, x], preferred_element_type=jnp.float32).astype(jnp.bfloat16)
            for x in range(2 * RING)
        ]
        tiles = swapped(tiles)
        for h in range(PARTS):
            for i in range(RING):
                s1[h, f, i] = tiles[h * RING + i]
        if f == 0:
            pl.semaphore_wait(barrier, RING - 1 + plane - 1 + 2)
        first(0, f)
    for f in range(frames):
        first(1, f)

    queries = owners.shape[1]
    small[1].wait()
    small[2].wait()
    mine = jnp.broadcast_to((owner_row[...] == group).astype(jnp.float32), (RING, queries))
    row = lax.broadcasted_iota(jnp.int32, (queries, queries), 0)
    column = lax.broadcasted_iota(jnp.int32, (queries, queries), 1)
    triangle = (row < column).astype(jnp.bfloat16)
    rank = jnp.dot(mine.astype(jnp.bfloat16), triangle, preferred_element_type=jnp.float32)
    slot = lax.broadcasted_iota(jnp.int32, (RING, queries), 0).astype(jnp.float32)
    picked = jnp.where(rank == slot, mine, 0.0).astype(jnp.bfloat16)
    cells_of = [shift_in[f, seat] for f in range(frames)]

    def second(h):
        for f in range(frames):
            landed(s1.at[h, f], r1.at[h, f], z, recv1.at[h, f], own1.at[h, f])
            s2[h, f] = jnp.swapaxes(r1[h, f], 0, 1)
            spread(s2.at[h, f], r2.at[h, f], spot, at_spot, send2.at[h, f], recv2.at[h, f], own2.at[h, f])

    lane = lax.broadcasted_iota(jnp.int32, (128, LANES), 1)

    def third(h):
        for f in range(frames):
            landed(s2.at[h, f], r2.at[h, f], spot, recv2.at[h, f], own2.at[h, f])
            for i in range(RING):
                part = r2[h, f, i].astype(jnp.float32)
                at = (i // 2) * RING
                long[h, f, i % 2, at:at + RING] = part
                long[h, f, i % 2, 128 + at:128 + at + RING] = part
        for j in range(2):
            total = None
            for f in range(frames):
                rows = cells_of[f] // 32
                turn = (cells_of[f] % 32) * WIDE

                def moved(rows):
                    low = rows % 2
                    down = (rows // 2 + (j < low).astype(jnp.int32)) % 128
                    return long[h, f, (j + 2 - low) % 2, pl.ds(128 - down, 128), :]

                both = jnp.where(lane >= LANES - turn, moved(rows + 1), moved(rows))
                both = pltpu.roll(both, turn, 1)
                total = both if total is None else total + both
            total = total.astype(jnp.bfloat16)
            for i in range(8):
                s3[h, i * 2 + j] = total[i * RING:(i + 1) * RING]
        pltpu.make_async_copy(s3.at[h, spot], r3.at[h, seat], own3.at[h]).start()

        def one(d, carry):
            i = (seat + d) % plane
            pltpu.make_async_remote_copy(
                src_ref=s3.at[h, i % RING], dst_ref=r3.at[h, seat], send_sem=send3.at[h], recv_sem=recv3.at[h],
                device_id=in_plane(i), device_id_type=MESH,
            ).start()
            return carry

        lax.fori_loop(1, plane, one, 0)

    def fourth(h):
        pltpu.make_async_copy(s3.at[h, spot], r3.at[h, seat], own3.at[h]).wait()
        most = r3.at[h, pl.ds(0, plane - 1)]
        pltpu.make_async_copy(most, most, recv3.at[h]).wait()
        sums = jnp.swapaxes(r3[h], 0, 1)
        for i in range(RING):
            s4[h, i] = jnp.dot(picked, sums[i], preferred_element_type=jnp.float32).astype(jnp.bfloat16)
        spread(s4.at[h], r4.at[h], z, at_z, send4.at[h], recv4.at[h], own4.at[h])

    second(0)
    third(0)
    second(1)
    fourth(0)
    third(1)
    fourth(1)
    for h in range(PARTS):
        landed(s4.at[h], r4.at[h], z, recv4.at[h], own4.at[h])
    tiles = swapped([r4[h, i] for h in range(PARTS) for i in range(RING)])
    for x in range(2 * RING):
        field[1 + x] = tiles[x]

    length = 2 * RING
    up = pltpu.make_async_remote_copy(
        src_ref=field.at[length], dst_ref=field.at[0], send_sem=halo_send.at[0], recv_sem=halo_recv.at[0],
        device_id={"loop": after}, device_id_type=MESH,
    )
    down = pltpu.make_async_remote_copy(
        src_ref=field.at[1], dst_ref=field.at[length + 1], send_sem=halo_send.at[1], recv_sem=halo_recv.at[1],
        device_id={"loop": before}, device_id_type=MESH,
    )
    up.start()
    down.start()
    for h in range(PARTS):
        for f in range(frames):
            sent(s1.at[h, f], send1.at[h, f])
            sent(s2.at[h, f], send2.at[h, f])
        most = r3.at[h, pl.ds(0, plane - 1)]
        pltpu.make_async_copy(most, most, send3.at[h]).wait()
        sent(s4.at[h], send4.at[h])
    up.wait()
    down.wait()


def finish(field, recon, sensor):
    u = field[...].astype(jnp.float32)
    center, upper, lower = u[1:-1], u[2:], u[:-2]
    recon[...] = jnp.swapaxes(center, 0, 1)
    place = lax.broadcasted_iota(jnp.int32, center.shape, 2)
    right = jnp.where(place == LANES - 1, 0.0, pltpu.roll(center, LANES - 1, 2))
    left = jnp.where(place == 0, 0.0, pltpu.roll(center, 1, 2))
    numerator = jnp.abs(upper - 2.0 * center + lower) + jnp.abs(right - 2.0 * center + left)
    denominator = jnp.maximum(jnp.abs(upper) + 2.0 * jnp.abs(center) + jnp.abs(lower), 1.0)
    sensor[...] = jnp.swapaxes(numerator / denominator, 0, 1)


def shards(coefficients, mode_basis, shifts, owners):
    per_device = coefficients.shape[0]
    queries = owners.shape[0]
    frames, modes, rows, cells = mode_basis.shape
    bf16, f32 = jnp.bfloat16, jnp.float32
    block = (RING, RING, LANES)
    hbm = pl.BlockSpec(memory_space=pltpu.HBM)
    dma = pltpu.SemaphoreType.DMA
    field = pl.pallas_call(
        kernel,
        out_shape=jax.ShapeDtypeStruct((rows + 2, per_device, cells), bf16),
        in_specs=[hbm, hbm, hbm, hbm],
        out_specs=pl.BlockSpec(memory_space=pltpu.VMEM),
        scratch_shapes=[
            pltpu.SMEM((frames, queries), jnp.int32),
            pltpu.VMEM((1, queries), jnp.int32),
            pltpu.VMEM((frames, per_device, modes), bf16),
            pltpu.VMEM((frames, modes, rows, cells), bf16),
            pltpu.VMEM((frames, rows, modes, cells), bf16),
            pltpu.VMEM((PARTS, frames) + block, bf16),
            pltpu.VMEM((PARTS, frames) + block, bf16),
            pltpu.VMEM((PARTS, frames) + block, bf16),
            pltpu.VMEM((PARTS, frames) + block, bf16),
            pltpu.VMEM((PARTS, frames, 2, 256, LANES), f32),
            pltpu.VMEM((PARTS,) + block, bf16),
            pltpu.VMEM((PARTS, 2 * RING, RING, LANES), bf16),
            pltpu.VMEM((PARTS,) + block, bf16),
            pltpu.VMEM((PARTS,) + block, bf16),
            dma((frames,)), dma((3,)),
            dma((PARTS, frames)), dma((PARTS, frames)), dma((PARTS, frames)),
            dma((PARTS, frames)), dma((PARTS, frames)), dma((PARTS, frames)),
            dma((PARTS,)), dma((PARTS,)), dma((PARTS,)),
            dma((PARTS,)), dma((PARTS,)), dma((PARTS,)),
            dma((2,)), dma((2,)),
        ],
        compiler_params=pltpu.CompilerParams(
            collective_id=0, has_side_effects=True, vmem_limit_bytes=63 * 1024 * 1024
        ),
    )(jnp.swapaxes(coefficients, 0, 1), mode_basis, shifts.T, owners.reshape(1, queries))
    part = 8
    out = pl.BlockSpec((part, rows, cells), lambda i: (i, 0, 0))
    recon, sensor = pl.pallas_call(
        finish,
        grid=(per_device // part,),
        out_shape=[jax.ShapeDtypeStruct((per_device, rows, cells), f32)] * 2,
        in_specs=[pl.BlockSpec((rows + 2, part, cells), lambda i: (0, i, 0))],
        out_specs=[out, out],
        compiler_params=pltpu.CompilerParams(vmem_limit_bytes=63 * 1024 * 1024),
    )(field)
    return recon, sensor


def solution(mesh):
    placed = (P("query", None, None), P(None, None, "loop", None), P(), P())
    return jax.shard_map(
        shards,
        mesh=mesh,
        in_specs=placed,
        out_specs=(P("query", "loop", None), P("query", "loop", None)),
        check_vma=False,
    )
```

```python
import functools

import jax
import jax.numpy as jnp
from jax import lax
from jax.experimental import pallas as pl
from jax.experimental.pallas import tpu as pltpu
from jax.sharding import PartitionSpec as P

MESH = pl.DeviceIdType.MESH
RING = 16
LANES = 128
WIDE = 4
PARTS = 2


def swapped(tiles):
    lane = lax.broadcasted_iota(jnp.int32, tiles[0].shape, 1)
    count = len(tiles)
    step = 1
    while step < count:
        width = step * (LANES // count)
        low = (lane // width) % 2 == 0
        new = [None] * count
        for i in range(count):
            if i & step:
                continue
            a, b = tiles[i], tiles[i | step]
            new[i] = jnp.where(low, a, pltpu.roll(b, width, 1))
            new[i | step] = jnp.where(low, pltpu.roll(a, LANES - width, 1), b)
        tiles = new
        step = step * 2
    return tiles


def kernel(
    coef, basis, shifts, owners, field,
    rows_in, shift_in, owner_row, coefs, raw, modes, s1, r1, s2, r2, long, s3, r3, s4, r4,
    p1, q1, p2, q2, p3, q3, p4, q4,
    basis_sem, small_sem, field_sem, send1, recv1, own1, send2, recv2, own2,
    send3, recv3, own3, send4, recv4, own4, halo_send, halo_recv,
):
    me = lax.axis_index("loop")
    group = lax.axis_index("query")
    devices = lax.axis_size("loop")
    core = me % 2
    z = (me // 2) % RING
    sup = me // (2 * RING)
    spot = sup * 2 + core
    before = (me + devices - 1) % devices
    after = (me + 1) % devices

    def at_z(i):
        return sup * (2 * RING) + i * 2 + core

    def at_spot(i):
        return (i // 2) * (2 * RING) + z * 2 + i % 2

    plane = 2 * RING
    seat = group * RING + spot

    def in_plane(i):
        return {"loop": at_spot(i % RING), "query": i // RING}

    def farthest_first(k):
        return RING // 2 + (1 - 2 * (k % 2)) * ((k + 1) // 2)

    barrier = pltpu.get_barrier_semaphore()

    def greet_z(k, carry):
        i = (z + farthest_first(k)) % RING
        pl.semaphore_signal(barrier, inc=1, device_id={"loop": at_z(i)}, device_id_type=MESH)
        return carry

    def greet_plane(d, carry):
        pl.semaphore_signal(barrier, inc=1, device_id=in_plane((seat + d) % plane), device_id_type=MESH)
        return carry

    lax.fori_loop(0, RING - 1, greet_z, 0)
    lax.fori_loop(1, plane, greet_plane, 0)
    pl.semaphore_signal(barrier, inc=1, device_id={"loop": before}, device_id_type=MESH)
    pl.semaphore_signal(barrier, inc=1, device_id={"loop": after}, device_id_type=MESH)

    frames = basis.shape[0]
    small = [
        pltpu.make_async_copy(coef, coefs, small_sem.at[0]),
        pltpu.make_async_copy(owners, owner_row, small_sem.at[1]),
        pltpu.make_async_copy(shifts, shift_in, small_sem.at[2]),
    ]
    loads = [pltpu.make_async_copy(basis.at[f], raw.at[f], basis_sem.at[f]) for f in range(frames)]
    loads[0].start()
    for load in small + loads[1:]:
        load.start()

    def spread(source, target, here, to, send_sem, recv_sem, own_sem):
        pltpu.make_async_copy(source.at[here], target.at[here], own_sem).start()

        def one(k, carry):
            i = (here + farthest_first(k)) % RING
            pltpu.make_async_remote_copy(
                src_ref=source.at[i], dst_ref=target.at[here], send_sem=send_sem, recv_sem=recv_sem,
                device_id={"loop": to(i)}, device_id_type=MESH,
            ).start()
            return carry

        lax.fori_loop(0, RING - 1, one, 0)

    def landed(source, target, here, recv_sem, own_sem):
        pltpu.make_async_copy(source.at[here], target.at[here], own_sem).wait()
        most = target.at[pl.ds(0, RING - 1)]
        pltpu.make_async_copy(most, most, recv_sem).wait()

    def sent(source, send_sem):
        most = source.at[pl.ds(0, RING - 1)]
        pltpu.make_async_copy(most, most, send_sem).wait()

    def first(h, f):
        spread(s1.at[h, f], r1.at[h, f], z, at_z, send1.at[h, f], recv1.at[h, f], own1.at[h, f])

    def spread_plane(source, target, send_sem, recv_sem, own_sem):
        pltpu.make_async_copy(source.at[spot], target.at[seat], own_sem).start()

        def one(d, carry):
            i = (seat + d) % plane
            pltpu.make_async_remote_copy(
                src_ref=source.at[i % RING], dst_ref=target.at[seat], send_sem=send_sem, recv_sem=recv_sem,
                device_id=in_plane(i), device_id_type=MESH,
            ).start()
            return carry

        lax.fori_loop(1, plane, one, 0)

    def landed_plane(source, target, recv_sem, own_sem):
        pltpu.make_async_copy(source.at[spot], target.at[seat], own_sem).wait()
        most = target.at[pl.ds(0, plane - 1)]
        pltpu.make_async_copy(most, most, recv_sem).wait()

    def sent_plane(target, send_sem):
        most = target.at[pl.ds(0, plane - 1)]
        pltpu.make_async_copy(most, most, send_sem).wait()

    last = frames
    for f in range(frames):
        loads[f].wait()
        modes[f] = jnp.swapaxes(raw[f], 0, 1)
        if f == 0:
            small[0].wait()
        weights = coefs[f]
        tiles = [
            jnp.dot(weights, modes[f, x], preferred_element_type=jnp.float32).astype(jnp.bfloat16)
            for x in range(2 * RING)
        ]
        tiles = swapped(tiles)
        for i in range(RING):
            s1[f, i] = tiles[i]
        if f == 0:
            pl.semaphore_wait(barrier, RING - 1 + plane - 1 + 2)
        spread(s1.at[f], r1.at[f], z, at_z, send1.at[f], recv1.at[f], own1.at[f])
        p1[:, f] = jnp.swapaxes(jnp.stack(tiles[RING:]), 0, 1)
    spread(p1, q1, spot, at_spot, send2.at[last], recv2.at[last], own2.at[last])

    queries = owners.shape[1]
    small[1].wait()
    small[2].wait()
    mine = jnp.broadcast_to((owner_row[...] == group).astype(jnp.float32), (RING, queries))
    row = lax.broadcasted_iota(jnp.int32, (queries, queries), 0)
    column = lax.broadcasted_iota(jnp.int32, (queries, queries), 1)
    triangle = (row < column).astype(jnp.bfloat16)
    rank = jnp.dot(mine.astype(jnp.bfloat16), triangle, preferred_element_type=jnp.float32)
    slot = lax.broadcasted_iota(jnp.int32, (RING, queries), 0).astype(jnp.float32)
    picked = jnp.where(rank == slot, mine, 0.0).astype(jnp.bfloat16)
    cells_of = [shift_in[f, seat] for f in range(frames)]

    lane = lax.broadcasted_iota(jnp.int32, (128, LANES), 1)

    def store_long(h, f, i, part):
        part = part.astype(jnp.float32)
        at = (i // 2) * RING
        long[h, f, i % 2, at:at + RING] = part
        long[h, f, i % 2, 128 + at:128 + at + RING] = part

    def summed(h):
        sums = []
        for j in range(2):
            total = None
            for f in range(frames):
                rows = cells_of[f] // 32
                turn = (cells_of[f] % 32) * WIDE

                def moved(rows):
                    low = rows % 2
                    down = (rows // 2 + (j < low).astype(jnp.int32)) % 128
                    return long[h, f, (j + 2 - low) % 2, pl.ds(128 - down, 128), :]

                both = jnp.where(lane >= LANES - turn, moved(rows + 1), moved(rows))
                both = pltpu.roll(both, turn, 1)
                total = both if total is None else total + both
            sums.append(total.astype(jnp.bfloat16))
        return [sums[i % 2][(i // 2) * RING:(i // 2 + 1) * RING] for i in range(RING)]

    def owned(blocks):
        blocks = jnp.swapaxes(blocks, 0, 1)
        return [
            jnp.dot(picked, blocks[i], preferred_element_type=jnp.float32).astype(jnp.bfloat16)
            for i in range(RING)
        ]

    landed(p1, q1, spot, recv2.at[last], own2.at[last])
    for f in range(frames):
        p2[:, f] = jnp.swapaxes(q1[:, f], 0, 1)
    spread(p2, q2, z, at_z, send1.at[last], recv1.at[last], own1.at[last])

    for f in range(frames):
        landed(s1.at[f], r1.at[f], z, recv1.at[f], own1.at[f])
        s2[f] = jnp.swapaxes(r1[f], 0, 1)
        spread(s2.at[f], r2.at[f], spot, at_spot, send2.at[f], recv2.at[f], own2.at[f])
    for f in range(frames):
        landed(s2.at[f], r2.at[f], spot, recv2.at[f], own2.at[f])
        for i in range(RING):
            store_long(0, f, i, r2[f, i])
    parts = summed(0)
    for i in range(RING):
        s3[i] = parts[i]
    spread_plane(s3, r3, send3.at[0], recv3.at[0], own3.at[0])

    landed(p2, q2, z, recv1.at[last], own1.at[last])
    for f in range(frames):
        blocks = jnp.swapaxes(q2[:, f], 0, 1)
        for i in range(RING):
            store_long(1, f, i, blocks[i])
    p3[...] = jnp.swapaxes(jnp.stack(summed(1)), 0, 1)
    spread(p3, q3, z, at_z, send4.at[1], recv4.at[1], own4.at[1])

    landed_plane(s3, r3, recv3.at[0], own3.at[0])
    parts = owned(r3[...])
    for i in range(RING):
        s4[i] = parts[i]
    spread(s4, r4, z, at_z, send4.at[0], recv4.at[0], own4.at[0])

    landed(p3, q3, z, recv4.at[1], own4.at[1])
    p4[...] = jnp.swapaxes(q3[...], 0, 1)
    spread_plane(p4, q4, send3.at[1], recv3.at[1], own3.at[1])

    landed(s4, r4, z, recv4.at[0], own4.at[0])
    landed_plane(p4, q4, recv3.at[1], own3.at[1])
    tiles = swapped([r4[i] for i in range(RING)] + owned(q4[...]))
    for x in range(2 * RING):
        rows_in[x] = tiles[x]

    length = 2 * RING
    up = pltpu.make_async_remote_copy(
        src_ref=rows_in.at[length - 1], dst_ref=field.at[0], send_sem=halo_send.at[0], recv_sem=halo_recv.at[0],
        device_id={"loop": after}, device_id_type=MESH,
    )
    down = pltpu.make_async_remote_copy(
        src_ref=rows_in.at[0], dst_ref=field.at[length + 1], send_sem=halo_send.at[1], recv_sem=halo_recv.at[1],
        device_id={"loop": before}, device_id_type=MESH,
    )
    up.start()
    down.start()
    inside = pltpu.make_async_copy(rows_in, field.at[pl.ds(1, length)], field_sem)
    inside.start()
    for f in range(frames):
        sent(s1.at[f], send1.at[f])
        sent(s2.at[f], send2.at[f])
    sent(p1, send2.at[last])
    sent(p2, send1.at[last])
    sent_plane(r3, send3.at[0])
    sent(s4, send4.at[0])
    sent(p3, send4.at[1])
    sent_plane(q4, send3.at[1])
    inside.wait()
    up.wait()
    down.wait()


def finish(field, recon, sensor):
    u = field[...].astype(jnp.float32)
    center, upper, lower = u[1:-1], u[2:], u[:-2]
    recon[...] = jnp.swapaxes(center, 0, 1)
    place = lax.broadcasted_iota(jnp.int32, center.shape, 2)
    right = jnp.where(place == LANES - 1, 0.0, pltpu.roll(center, LANES - 1, 2))
    left = jnp.where(place == 0, 0.0, pltpu.roll(center, 1, 2))
    numerator = jnp.abs(upper - 2.0 * center + lower) + jnp.abs(right - 2.0 * center + left)
    denominator = jnp.maximum(jnp.abs(upper) + 2.0 * jnp.abs(center) + jnp.abs(lower), 1.0)
    sensor[...] = jnp.swapaxes(numerator / denominator, 0, 1)


def shards(coefficients, mode_basis, shifts, owners):
    per_device = coefficients.shape[0]
    queries = owners.shape[0]
    frames, modes, rows, cells = mode_basis.shape
    bf16, f32 = jnp.bfloat16, jnp.float32
    block = (RING, RING, LANES)
    hbm = pl.BlockSpec(memory_space=pltpu.HBM)
    dma = pltpu.SemaphoreType.DMA
    field = pl.pallas_call(
        kernel,
        out_shape=jax.ShapeDtypeStruct((rows + 2, per_device, cells), bf16),
        in_specs=[hbm, hbm, hbm, hbm],
        out_specs=hbm,
        scratch_shapes=[
            pltpu.VMEM((rows, per_device, cells), bf16),
            pltpu.SMEM((frames, queries), jnp.int32),
            pltpu.VMEM((1, queries), jnp.int32),
            pltpu.VMEM((frames, per_device, modes), bf16),
            pltpu.VMEM((frames, modes, rows, cells), bf16),
            pltpu.VMEM((frames, rows, modes, cells), bf16),
            pltpu.VMEM((frames,) + block, bf16),
            pltpu.VMEM((frames,) + block, bf16),
            pltpu.VMEM((frames,) + block, bf16),
            pltpu.VMEM((frames,) + block, bf16),
            pltpu.VMEM((PARTS, frames, 2, 256, LANES), f32),
            pltpu.VMEM(block, bf16),
            pltpu.VMEM((2 * RING, RING, LANES), bf16),
            pltpu.VMEM(block, bf16),
            pltpu.VMEM(block, bf16),
            pltpu.VMEM((RING, frames, RING, LANES), bf16),
            pltpu.VMEM((RING, frames, RING, LANES), bf16),
            pltpu.VMEM((RING, frames, RING, LANES), bf16),
            pltpu.VMEM((RING, frames, RING, LANES), bf16),
            pltpu.VMEM(block, bf16),
            pltpu.VMEM(block, bf16),
            pltpu.VMEM(block, bf16),
            pltpu.VMEM((2 * RING, RING, LANES), bf16),
            dma((frames,)), dma((3,)), dma(()),
            dma((frames + 1,)), dma((frames + 1,)), dma((frames + 1,)),
            dma((frames + 1,)), dma((frames + 1,)), dma((frames + 1,)),
            dma((PARTS,)), dma((PARTS,)), dma((PARTS,)),
            dma((PARTS,)), dma((PARTS,)), dma((PARTS,)),
            dma((2,)), dma((2,)),
        ],
        compiler_params=pltpu.CompilerParams(
            collective_id=0, has_side_effects=True, vmem_limit_bytes=63 * 1024 * 1024
        ),
    )(jnp.swapaxes(coefficients, 0, 1), mode_basis, shifts.T, owners.reshape(1, queries))
    part = 8
    out = pl.BlockSpec((part, rows, cells), lambda i: (i, 0, 0))
    recon, sensor = pl.pallas_call(
        finish,
        grid=(per_device // part,),
        out_shape=[jax.ShapeDtypeStruct((per_device, rows, cells), f32)] * 2,
        in_specs=[pl.BlockSpec((rows + 2, part, cells), lambda i: (0, i, 0))],
        out_specs=[out, out],
        compiler_params=pltpu.CompilerParams(vmem_limit_bytes=63 * 1024 * 1024),
    )(field)
    return recon, sensor


def solution(mesh):
    placed = (P("query", None, None), P(None, None, "loop", None), P(), P())
    return jax.shard_map(
        shards,
        mesh=mesh,
        in_specs=placed,
        out_specs=(P("query", "loop", None), P("query", "loop", None)),
        check_vma=False,
    )
```

```python
import functools

import jax
import jax.numpy as jnp
from jax import lax
from jax.experimental import pallas as pl
from jax.experimental.pallas import tpu as pltpu
from jax.sharding import PartitionSpec as P

MESH = pl.DeviceIdType.MESH
RING = 16
LANES = 128
WIDE = 4
PARTS = 2


def swapped(tiles, step=1, stop=2 * RING, blocks=2 * RING):
    lane = lax.broadcasted_iota(jnp.int32, tiles[0].shape, 1)
    count = len(tiles)
    while step < stop:
        width = step * (LANES // blocks)
        low = (lane // width) % 2 == 0
        new = [None] * count
        for i in range(count):
            if i & step:
                continue
            a, b = tiles[i], tiles[i | step]
            new[i] = jnp.where(low, a, pltpu.roll(b, width, 1))
            new[i | step] = jnp.where(low, pltpu.roll(a, LANES - width, 1), b)
        tiles = new
        step = step * 2
    return tiles


def kernel(
    coef, basis, shifts, owners, field,
    rows_in, edges, shift_in, owner_row, coefs, raw, modes, s1, r1, s2, r2, e1, f1, e2, f2, long, s3, r3, s4, r4,
    p1, q1, p2, q2, p3, q3, p4, q4,
    basis_sem, small_sem, field_sem, send1, recv1, own1, send2, recv2, own2,
    send3, recv3, own3, send4, recv4, own4, halo_send, halo_recv,
):
    me = lax.axis_index("loop")
    group = lax.axis_index("query")
    devices = lax.axis_size("loop")
    core = me % 2
    z = (me // 2) % RING
    sup = me // (2 * RING)
    spot = sup * 2 + core
    before = (me + devices - 1) % devices
    after = (me + 1) % devices

    def at_z(i):
        return sup * (2 * RING) + i * 2 + core

    def at_spot(i):
        return (i // 2) * (2 * RING) + z * 2 + i % 2

    plane = 2 * RING
    seat = group * RING + spot

    def in_plane(i):
        return {"loop": at_spot(i % RING), "query": i // RING}

    def farthest_first(k):
        return RING // 2 + (1 - 2 * (k % 2)) * ((k + 1) // 2)

    barrier = pltpu.get_barrier_semaphore()

    def greet_z(k, carry):
        i = (z + farthest_first(k)) % RING
        pl.semaphore_signal(barrier, inc=1, device_id={"loop": at_z(i)}, device_id_type=MESH)
        return carry

    def greet_plane(d, carry):
        pl.semaphore_signal(barrier, inc=1, device_id=in_plane((seat + d) % plane), device_id_type=MESH)
        return carry

    frames = basis.shape[0]
    loads = [pltpu.make_async_copy(basis.at[f], raw.at[f], basis_sem.at[f]) for f in range(frames)]
    small = [
        pltpu.make_async_copy(coef, coefs, small_sem.at[0]),
        pltpu.make_async_copy(owners, owner_row, small_sem.at[1]),
        pltpu.make_async_copy(shifts, shift_in, small_sem.at[2]),
    ]
    loads[0].start()
    small[0].start()
    lax.fori_loop(0, RING - 1, greet_z, 0, unroll=True)
    for load in loads[1:] + small[1:]:
        load.start()
    lax.fori_loop(1, plane, greet_plane, 0, unroll=True)
    pl.semaphore_signal(barrier, inc=1, device_id={"loop": before}, device_id_type=MESH)
    pl.semaphore_signal(barrier, inc=1, device_id={"loop": after}, device_id_type=MESH)

    def spread(source, target, here, to, send_sem, recv_sem, own_sem):
        pltpu.make_async_copy(source.at[here], target.at[here], own_sem).start()

        def one(k, carry):
            i = (here + farthest_first(k)) % RING
            pltpu.make_async_remote_copy(
                src_ref=source.at[i], dst_ref=target.at[here], send_sem=send_sem, recv_sem=recv_sem,
                device_id={"loop": to(i)}, device_id_type=MESH,
            ).start()
            return carry

        lax.fori_loop(0, RING - 1, one, 0, unroll=True)

    def landed(source, target, here, recv_sem, own_sem):
        pltpu.make_async_copy(source.at[here], target.at[here], own_sem).wait()
        most = target.at[pl.ds(0, RING - 1)]
        pltpu.make_async_copy(most, most, recv_sem).wait()

    def sent(source, send_sem):
        most = source.at[pl.ds(0, RING - 1)]
        pltpu.make_async_copy(most, most, send_sem).wait()

    def first(h, f):
        spread(s1.at[h, f], r1.at[h, f], z, at_z, send1.at[h, f], recv1.at[h, f], own1.at[h, f])

    def spread_plane(source, target, send_sem, recv_sem, own_sem):
        pltpu.make_async_copy(source.at[spot], target.at[seat], own_sem).start()

        def one(d, carry):
            i = (seat + d) % plane
            pltpu.make_async_remote_copy(
                src_ref=source.at[i % RING], dst_ref=target.at[seat], send_sem=send_sem, recv_sem=recv_sem,
                device_id=in_plane(i), device_id_type=MESH,
            ).start()
            return carry

        lax.fori_loop(1, plane, one, 0, unroll=True)

    def landed_plane(source, target, recv_sem, own_sem):
        pltpu.make_async_copy(source.at[spot], target.at[seat], own_sem).wait()
        most = target.at[pl.ds(0, plane - 1)]
        pltpu.make_async_copy(most, most, recv_sem).wait()

    def sent_plane(target, send_sem):
        most = target.at[pl.ds(0, plane - 1)]
        pltpu.make_async_copy(most, most, send_sem).wait()

    last = 2
    early = frames - 1
    trains = [(0, range(early), s1, r1, s2, r2), (1, range(early, frames), e1, f1, e2, f2)]
    for k, members, out, into, _, _ in trains:
        for f in members:
            loads[f].wait()
            modes[f] = jnp.swapaxes(raw[f], 0, 1)
            if f == 0:
                small[0].wait()
            weights = coefs[f]
            tiles = [
                jnp.dot(weights, modes[f, x], preferred_element_type=jnp.float32).astype(jnp.bfloat16)
                for x in range(2 * RING)
            ]
            tiles = swapped(tiles)
            for i in range(RING):
                out[i, f - members[0]] = tiles[i]
            p1[:, f] = jnp.swapaxes(jnp.stack(tiles[RING:]), 0, 1)
        if k == 0:
            pl.semaphore_wait(barrier, RING - 1 + plane - 1 + 2)
        spread(out, into, z, at_z, send1.at[k], recv1.at[k], own1.at[k])
    spread(p1, q1, spot, at_spot, send2.at[last], recv2.at[last], own2.at[last])

    queries = owners.shape[1]
    small[1].wait()
    small[2].wait()
    mine = jnp.broadcast_to((owner_row[...] == group).astype(jnp.float32), (RING, queries))
    row = lax.broadcasted_iota(jnp.int32, (queries, queries), 0)
    column = lax.broadcasted_iota(jnp.int32, (queries, queries), 1)
    triangle = (row < column).astype(jnp.bfloat16)
    rank = jnp.dot(mine.astype(jnp.bfloat16), triangle, preferred_element_type=jnp.float32)
    slot = lax.broadcasted_iota(jnp.int32, (RING, queries), 0).astype(jnp.float32)
    picked = jnp.where(rank == slot, mine, 0.0).astype(jnp.bfloat16)
    cells_of = [shift_in[f, seat] for f in range(frames)]

    lane = lax.broadcasted_iota(jnp.int32, (128, LANES), 1)

    def store_long(h, f, i, part):
        part = part.astype(jnp.float32)
        at = (i // 2) * RING
        long[h, f, i % 2, at:at + RING] = part
        long[h, f, i % 2, 128 + at:128 + at + RING] = part

    def summed(h):
        sums = []
        for j in range(2):
            total = None
            for f in range(frames):
                rows = cells_of[f] // 32
                turn = (cells_of[f] % 32) * WIDE

                def moved(rows):
                    low = rows % 2
                    down = (rows // 2 + (j < low).astype(jnp.int32)) % 128
                    return long[h, f, (j + 2 - low) % 2, pl.ds(128 - down, 128), :]

                both = jnp.where(lane >= LANES - turn, moved(rows + 1), moved(rows))
                both = pltpu.roll(both, turn, 1)
                total = both if total is None else total + both
            sums.append(total.astype(jnp.bfloat16))
        return [sums[i % 2][(i // 2) * RING:(i // 2 + 1) * RING] for i in range(RING)]

    def owned(blocks):
        blocks = jnp.swapaxes(blocks, 0, 1)
        return [
            jnp.dot(picked, blocks[i], preferred_element_type=jnp.float32).astype(jnp.bfloat16)
            for i in range(RING)
        ]

    landed(p1, q1, spot, recv2.at[last], own2.at[last])
    for f in range(frames):
        p2[:, f] = jnp.swapaxes(q1[:, f], 0, 1)
    spread(p2, q2, z, at_z, send1.at[last], recv1.at[last], own1.at[last])

    for k, members, out, into, out2, _ in trains:
        landed(out, into, z, recv1.at[k], own1.at[k])
        for n in range(len(members)):
            out2[:, n] = jnp.swapaxes(into[:, n], 0, 1)
        spread(out2, trains[k][5], spot, at_spot, send2.at[k], recv2.at[k], own2.at[k])
    for k, members, _, _, out2, into2 in trains:
        landed(out2, into2, spot, recv2.at[k], own2.at[k])
        for f in members:
            for i in range(RING):
                store_long(0, f, i, into2[i, f - members[0]])
    parts = summed(0)
    for i in range(RING):
        s3[i] = parts[i]
    spread_plane(s3, r3, send3.at[0], recv3.at[0], own3.at[0])

    landed(p2, q2, z, recv1.at[last], own1.at[last])
    for f in range(frames):
        blocks = jnp.swapaxes(q2[:, f], 0, 1)
        for i in range(RING):
            store_long(1, f, i, blocks[i])
    p3[...] = jnp.swapaxes(jnp.stack(summed(1)), 0, 1)
    spread(p3, q3, z, at_z, send4.at[1], recv4.at[1], own4.at[1])

    landed_plane(s3, r3, recv3.at[0], own3.at[0])
    parts = owned(r3[...])
    for i in range(RING):
        s4[i] = parts[i]
    spread(s4, r4, z, at_z, send4.at[0], recv4.at[0], own4.at[0])

    landed(p3, q3, z, recv4.at[1], own4.at[1])
    p4[...] = jnp.swapaxes(q3[...], 0, 1)
    spread_plane(p4, q4, send3.at[1], recv3.at[1], own3.at[1])

    length = 2 * RING
    place = lax.broadcasted_iota(jnp.int32, (RING, LANES), 1) // WIDE

    def edge(row, tiles, block, x):
        for i, tile in enumerate(tiles):
            row = jnp.where(place == block + i, pltpu.roll(tile, (block + i - x) * WIDE % LANES, 1), row)
        return row

    blank = jnp.zeros((RING, LANES), jnp.bfloat16)
    landed(s4, r4, z, recv4.at[0], own4.at[0])
    early_tiles = [r4[i] for i in range(RING)]
    first_row = edge(blank, early_tiles, 0, 0)
    last_row = edge(blank, early_tiles, 0, length - 1)
    early_tiles = swapped(early_tiles, 1, RING)
    landed_plane(p4, q4, recv3.at[1], own3.at[1])
    late_tiles = owned(q4[...])
    edges[0] = edge(first_row, late_tiles, RING, 0)
    edges[1] = edge(last_row, late_tiles, RING, length - 1)
    up = pltpu.make_async_remote_copy(
        src_ref=edges.at[1], dst_ref=field.at[0], send_sem=halo_send.at[0], recv_sem=halo_recv.at[0],
        device_id={"loop": after}, device_id_type=MESH,
    )
    down = pltpu.make_async_remote_copy(
        src_ref=edges.at[0], dst_ref=field.at[length + 1], send_sem=halo_send.at[1], recv_sem=halo_recv.at[1],
        device_id={"loop": before}, device_id_type=MESH,
    )
    up.start()
    down.start()
    tiles = swapped(early_tiles + swapped(late_tiles, 1, RING), RING, length)
    for x in range(length):
        rows_in[x] = tiles[x]
    inside = pltpu.make_async_copy(rows_in, field.at[pl.ds(1, length)], field_sem)
    inside.start()
    for k, _, out, _, out2, _ in trains:
        sent(out, send1.at[k])
        sent(out2, send2.at[k])
    sent(p1, send2.at[last])
    sent(p2, send1.at[last])
    sent_plane(r3, send3.at[0])
    sent(s4, send4.at[0])
    sent(p3, send4.at[1])
    sent_plane(q4, send3.at[1])
    inside.wait()
    up.wait()
    down.wait()


def finish(field, recon, sensor):
    u = field[...].astype(jnp.float32)
    center, upper, lower = u[1:-1], u[2:], u[:-2]
    recon[...] = jnp.swapaxes(center, 0, 1)
    place = lax.broadcasted_iota(jnp.int32, center.shape, 2)
    right = jnp.where(place == LANES - 1, 0.0, pltpu.roll(center, LANES - 1, 2))
    left = jnp.where(place == 0, 0.0, pltpu.roll(center, 1, 2))
    numerator = jnp.abs(upper - 2.0 * center + lower) + jnp.abs(right - 2.0 * center + left)
    denominator = jnp.maximum(jnp.abs(upper) + 2.0 * jnp.abs(center) + jnp.abs(lower), 1.0)
    sensor[...] = jnp.swapaxes(numerator / denominator, 0, 1)


def shards(coefficients, mode_basis, shifts, owners):
    per_device = coefficients.shape[0]
    queries = owners.shape[0]
    frames, modes, rows, cells = mode_basis.shape
    bf16, f32 = jnp.bfloat16, jnp.float32
    block = (RING, RING, LANES)
    hbm = pl.BlockSpec(memory_space=pltpu.HBM)
    dma = pltpu.SemaphoreType.DMA
    field = pl.pallas_call(
        kernel,
        out_shape=jax.ShapeDtypeStruct((rows + 2, per_device, cells), bf16),
        in_specs=[hbm, hbm, hbm, hbm],
        out_specs=hbm,
        scratch_shapes=[
            pltpu.VMEM((rows, per_device, cells), bf16),
            pltpu.VMEM((2, per_device, cells), bf16),
            pltpu.SMEM((frames, queries), jnp.int32),
            pltpu.VMEM((1, queries), jnp.int32),
            pltpu.VMEM((frames, per_device, modes), bf16),
            pltpu.VMEM((frames, modes, rows, cells), bf16),
            pltpu.VMEM((frames, rows, modes, cells), bf16),
            pltpu.VMEM((RING, frames - 1, RING, LANES), bf16),
            pltpu.VMEM((RING, frames - 1, RING, LANES), bf16),
            pltpu.VMEM((RING, frames - 1, RING, LANES), bf16),
            pltpu.VMEM((RING, frames - 1, RING, LANES), bf16),
            pltpu.VMEM((RING, 1, RING, LANES), bf16),
            pltpu.VMEM((RING, 1, RING, LANES), bf16),
            pltpu.VMEM((RING, 1, RING, LANES), bf16),
            pltpu.VMEM((RING, 1, RING, LANES), bf16),
            pltpu.VMEM((PARTS, frames, 2, 256, LANES), f32),
            pltpu.VMEM(block, bf16),
            pltpu.VMEM((2 * RING, RING, LANES), bf16),
            pltpu.VMEM(block, bf16),
            pltpu.VMEM(block, bf16),
            pltpu.VMEM((RING, frames, RING, LANES), bf16),
            pltpu.VMEM((RING, frames, RING, LANES), bf16),
            pltpu.VMEM((RING, frames, RING, LANES), bf16),
            pltpu.VMEM((RING, frames, RING, LANES), bf16),
            pltpu.VMEM(block, bf16),
            pltpu.VMEM(block, bf16),
            pltpu.VMEM(block, bf16),
            pltpu.VMEM((2 * RING, RING, LANES), bf16),
            dma((frames,)), dma((3,)), dma(()),
            dma((3,)), dma((3,)), dma((3,)),
            dma((3,)), dma((3,)), dma((3,)),
            dma((PARTS,)), dma((PARTS,)), dma((PARTS,)),
            dma((PARTS,)), dma((PARTS,)), dma((PARTS,)),
            dma((2,)), dma((2,)),
        ],
        compiler_params=pltpu.CompilerParams(
            collective_id=0, has_side_effects=True, vmem_limit_bytes=63 * 1024 * 1024
        ),
    )(jnp.swapaxes(coefficients, 0, 1), mode_basis, shifts.T, owners.reshape(1, queries))
    part = 8
    out = pl.BlockSpec((part, rows, cells), lambda i: (i, 0, 0))
    recon, sensor = pl.pallas_call(
        finish,
        grid=(per_device // part,),
        out_shape=[jax.ShapeDtypeStruct((per_device, rows, cells), f32)] * 2,
        in_specs=[pl.BlockSpec((rows + 2, part, cells), lambda i: (0, i, 0))],
        out_specs=[out, out],
        compiler_params=pltpu.CompilerParams(vmem_limit_bytes=63 * 1024 * 1024),
    )(field)
    return recon, sensor


def solution(mesh):
    placed = (P("query", None, None), P(None, None, "loop", None), P(), P())
    return jax.shard_map(
        shards,
        mesh=mesh,
        in_specs=placed,
        out_specs=(P("query", "loop", None), P("query", "loop", None)),
        check_vma=False,
    )
```

```python
import functools

import jax
import jax.numpy as jnp
from jax import lax
from jax.experimental import pallas as pl
from jax.experimental.pallas import tpu as pltpu
from jax.sharding import PartitionSpec as P

MESH = pl.DeviceIdType.MESH
RING = 16
LANES = 128
WIDE = 4
PARTS = 2


def swapped(tiles, step=1, stop=2 * RING, blocks=2 * RING):
    lane = lax.broadcasted_iota(jnp.int32, tiles[0].shape, 1)
    count = len(tiles)
    while step < stop:
        width = step * (LANES // blocks)
        low = (lane // width) % 2 == 0
        new = [None] * count
        for i in range(count):
            if i & step:
                continue
            a, b = tiles[i], tiles[i | step]
            new[i] = jnp.where(low, a, pltpu.roll(b, width, 1))
            new[i | step] = jnp.where(low, pltpu.roll(a, LANES - width, 1), b)
        tiles = new
        step = step * 2
    return tiles


def kernel(
    coef, basis, shifts, owners, field,
    rows_in, edges, shift_in, owner_row, coefs, raw, modes, s1, r1, s2, r2, e1, f1, e2, f2, long, s3, r3, s4, r4,
    p1, q1, p2, q2, p3, q3, p4, q4,
    basis_sem, small_sem, field_sem, send1, recv1, own1, send2, recv2, own2,
    send3, recv3, own3, send4, recv4, own4, halo_send, halo_recv,
):
    me = lax.axis_index("loop")
    group = lax.axis_index("query")
    devices = lax.axis_size("loop")
    core = me % 2
    z = (me // 2) % RING
    sup = me // (2 * RING)
    spot = sup * 2 + core
    before = (me + devices - 1) % devices
    after = (me + 1) % devices

    def at_z(i):
        return sup * (2 * RING) + i * 2 + core

    def at_spot(i):
        return (i // 2) * (2 * RING) + z * 2 + i % 2

    plane = 2 * RING
    seat = group * RING + spot

    def in_plane(i):
        return {"loop": at_spot(i % RING), "query": i // RING}

    def farthest_first(k):
        return RING // 2 + (1 - 2 * (k % 2)) * ((k + 1) // 2)

    barrier = pltpu.get_barrier_semaphore()

    def greet_z(k, carry):
        i = (z + farthest_first(k)) % RING
        pl.semaphore_signal(barrier, inc=1, device_id={"loop": at_z(i)}, device_id_type=MESH)
        return carry

    def greet_plane(d, carry):
        pl.semaphore_signal(barrier, inc=1, device_id=in_plane((seat + d) % plane), device_id_type=MESH)
        return carry

    frames = basis.shape[0]
    loads = [pltpu.make_async_copy(basis.at[f], raw.at[f], basis_sem.at[f]) for f in range(frames)]
    small = [
        pltpu.make_async_copy(coef, coefs, small_sem.at[0]),
        pltpu.make_async_copy(owners, owner_row, small_sem.at[1]),
        pltpu.make_async_copy(shifts, shift_in, small_sem.at[2]),
    ]
    loads[0].start()
    small[0].start()
    lax.fori_loop(0, RING - 1, greet_z, 0, unroll=True)
    for load in loads[1:] + small[1:]:
        load.start()
    lax.fori_loop(1, plane, greet_plane, 0, unroll=True)
    pl.semaphore_signal(barrier, inc=1, device_id={"loop": before}, device_id_type=MESH)
    pl.semaphore_signal(barrier, inc=1, device_id={"loop": after}, device_id_type=MESH)

    def spread(source, target, here, to, send_sem, recv_sem, own_sem):
        pltpu.make_async_copy(source.at[here], target.at[here], own_sem).start()

        def one(k, carry):
            i = (here + farthest_first(k)) % RING
            pltpu.make_async_remote_copy(
                src_ref=source.at[i], dst_ref=target.at[here], send_sem=send_sem, recv_sem=recv_sem,
                device_id={"loop": to(i)}, device_id_type=MESH,
            ).start()
            return carry

        lax.fori_loop(0, RING - 1, one, 0, unroll=True)

    def landed(source, target, here, recv_sem, own_sem):
        pltpu.make_async_copy(source.at[here], target.at[here], own_sem).wait()
        most = target.at[pl.ds(0, RING - 1)]
        pltpu.make_async_copy(most, most, recv_sem).wait()

    def sent(source, send_sem):
        most = source.at[pl.ds(0, RING - 1)]
        pltpu.make_async_copy(most, most, send_sem).wait()

    def first(h, f):
        spread(s1.at[h, f], r1.at[h, f], z, at_z, send1.at[h, f], recv1.at[h, f], own1.at[h, f])

    def spread_plane(source, target, send_sem, recv_sem, own_sem):
        pltpu.make_async_copy(source.at[spot], target.at[seat], own_sem).start()

        def one(d, carry):
            i = (seat + d) % plane
            pltpu.make_async_remote_copy(
                src_ref=source.at[i % RING], dst_ref=target.at[seat], send_sem=send_sem, recv_sem=recv_sem,
                device_id=in_plane(i), device_id_type=MESH,
            ).start()
            return carry

        lax.fori_loop(1, plane, one, 0, unroll=True)

    def landed_plane(source, target, recv_sem, own_sem):
        pltpu.make_async_copy(source.at[spot], target.at[seat], own_sem).wait()
        most = target.at[pl.ds(0, plane - 1)]
        pltpu.make_async_copy(most, most, recv_sem).wait()

    def sent_plane(target, send_sem):
        most = target.at[pl.ds(0, plane - 1)]
        pltpu.make_async_copy(most, most, send_sem).wait()

    last = 2
    early = frames - 1
    trains = [(0, range(early), s1, r1, s2, r2), (1, range(early, frames), e1, f1, e2, f2)]
    for k, members, out, into, _, _ in trains:
        for f in members:
            loads[f].wait()
            modes[f] = jnp.swapaxes(raw[f], 0, 1)
            if f == 0:
                small[0].wait()
            weights = coefs[f]
            tiles = [
                jnp.dot(weights, modes[f, x], preferred_element_type=jnp.float32).astype(jnp.bfloat16)
                for x in range(2 * RING)
            ]
            tiles = swapped(tiles)
            for i in range(RING):
                out[i, f - members[0]] = tiles[i]
            p1[:, f] = jnp.swapaxes(jnp.stack(tiles[RING:]), 0, 1)
        if k == 0:
            pl.semaphore_wait(barrier, RING - 1 + plane - 1 + 2)
        else:
            spread(p1, q1, spot, at_spot, send2.at[last], recv2.at[last], own2.at[last])
        spread(out, into, z, at_z, send1.at[k], recv1.at[k], own1.at[k])

    queries = owners.shape[1]
    small[1].wait()
    small[2].wait()
    mine = jnp.broadcast_to((owner_row[...] == group).astype(jnp.float32), (RING, queries))
    row = lax.broadcasted_iota(jnp.int32, (queries, queries), 0)
    column = lax.broadcasted_iota(jnp.int32, (queries, queries), 1)
    triangle = (row < column).astype(jnp.bfloat16)
    rank = jnp.dot(mine.astype(jnp.bfloat16), triangle, preferred_element_type=jnp.float32)
    slot = lax.broadcasted_iota(jnp.int32, (RING, queries), 0).astype(jnp.float32)
    picked = jnp.where(rank == slot, mine, 0.0).astype(jnp.bfloat16)
    cells_of = [shift_in[f, seat] for f in range(frames)]

    lane = lax.broadcasted_iota(jnp.int32, (128, LANES), 1)

    def store_long(h, f, i, part):
        part = part.astype(jnp.float32)
        at = (i // 2) * RING
        long[h, f, i % 2, at:at + RING] = part
        long[h, f, i % 2, 128 + at:128 + at + RING] = part

    def summed(h):
        sums = []
        for j in range(2):
            total = None
            for f in range(frames):
                rows = cells_of[f] // 32
                turn = (cells_of[f] % 32) * WIDE

                def moved(rows):
                    low = rows % 2
                    down = (rows // 2 + (j < low).astype(jnp.int32)) % 128
                    return long[h, f, (j + 2 - low) % 2, pl.ds(128 - down, 128), :]

                both = jnp.where(lane >= LANES - turn, moved(rows + 1), moved(rows))
                both = pltpu.roll(both, turn, 1)
                total = both if total is None else total + both
            sums.append(total.astype(jnp.bfloat16))
        return [sums[i % 2][(i // 2) * RING:(i // 2 + 1) * RING] for i in range(RING)]

    def owned(blocks):
        blocks = jnp.swapaxes(blocks, 0, 1)
        return [
            jnp.dot(picked, blocks[i], preferred_element_type=jnp.float32).astype(jnp.bfloat16)
            for i in range(RING)
        ]

    landed(p1, q1, spot, recv2.at[last], own2.at[last])
    for f in range(frames):
        p2[:, f] = jnp.swapaxes(q1[:, f], 0, 1)
    spread(p2, q2, z, at_z, send1.at[last], recv1.at[last], own1.at[last])

    for k, members, out, into, out2, _ in trains:
        landed(out, into, z, recv1.at[k], own1.at[k])
        for n in range(len(members)):
            out2[:, n] = jnp.swapaxes(into[:, n], 0, 1)
        spread(out2, trains[k][5], spot, at_spot, send2.at[k], recv2.at[k], own2.at[k])
    for k, members, _, _, out2, into2 in trains:
        landed(out2, into2, spot, recv2.at[k], own2.at[k])
        for f in members:
            for i in range(RING):
                store_long(0, f, i, into2[i, f - members[0]])
    parts = summed(0)
    for i in range(RING):
        s3[i] = parts[i]
    spread_plane(s3, r3, send3.at[0], recv3.at[0], own3.at[0])

    landed(p2, q2, z, recv1.at[last], own1.at[last])
    for f in range(frames):
        blocks = jnp.swapaxes(q2[:, f], 0, 1)
        for i in range(RING):
            store_long(1, f, i, blocks[i])
    p3[...] = jnp.swapaxes(jnp.stack(summed(1)), 0, 1)
    spread(p3, q3, z, at_z, send4.at[1], recv4.at[1], own4.at[1])

    landed_plane(s3, r3, recv3.at[0], own3.at[0])
    parts = owned(r3[...])
    for i in range(RING):
        s4[i] = parts[i]
    spread(s4, r4, z, at_z, send4.at[0], recv4.at[0], own4.at[0])

    landed(p3, q3, z, recv4.at[1], own4.at[1])
    p4[...] = jnp.swapaxes(q3[...], 0, 1)
    spread_plane(p4, q4, send3.at[1], recv3.at[1], own3.at[1])

    length = 2 * RING
    place = lax.broadcasted_iota(jnp.int32, (RING, LANES), 1) // WIDE

    def edge(row, tiles, block, x):
        for i, tile in enumerate(tiles):
            row = jnp.where(place == block + i, pltpu.roll(tile, (block + i - x) * WIDE % LANES, 1), row)
        return row

    blank = jnp.zeros((RING, LANES), jnp.bfloat16)
    landed(s4, r4, z, recv4.at[0], own4.at[0])
    early_tiles = [r4[i] for i in range(RING)]
    first_row = edge(blank, early_tiles, 0, 0)
    last_row = edge(blank, early_tiles, 0, length - 1)
    early_tiles = swapped(early_tiles, 1, RING)
    landed_plane(p4, q4, recv3.at[1], own3.at[1])
    late_tiles = owned(q4[...])
    edges[0] = edge(first_row, late_tiles, RING, 0)
    edges[1] = edge(last_row, late_tiles, RING, length - 1)
    up = pltpu.make_async_remote_copy(
        src_ref=edges.at[1], dst_ref=field.at[0], send_sem=halo_send.at[0], recv_sem=halo_recv.at[0],
        device_id={"loop": after}, device_id_type=MESH,
    )
    down = pltpu.make_async_remote_copy(
        src_ref=edges.at[0], dst_ref=field.at[length + 1], send_sem=halo_send.at[1], recv_sem=halo_recv.at[1],
        device_id={"loop": before}, device_id_type=MESH,
    )
    up.start()
    down.start()
    tiles = swapped(early_tiles + swapped(late_tiles, 1, RING), RING, length)
    for x in range(length):
        rows_in[x] = tiles[x]
    inside = pltpu.make_async_copy(rows_in, field.at[pl.ds(1, length)], field_sem)
    inside.start()
    for k, _, out, _, out2, _ in trains:
        sent(out, send1.at[k])
        sent(out2, send2.at[k])
    sent(p1, send2.at[last])
    sent(p2, send1.at[last])
    sent_plane(r3, send3.at[0])
    sent(s4, send4.at[0])
    sent(p3, send4.at[1])
    sent_plane(q4, send3.at[1])
    inside.wait()
    up.wait()
    down.wait()


def finish(field, recon, sensor):
    u = field[...].astype(jnp.float32)
    center, upper, lower = u[1:-1], u[2:], u[:-2]
    recon[...] = jnp.swapaxes(center, 0, 1)
    place = lax.broadcasted_iota(jnp.int32, center.shape, 2)
    right = jnp.where(place == LANES - 1, 0.0, pltpu.roll(center, LANES - 1, 2))
    left = jnp.where(place == 0, 0.0, pltpu.roll(center, 1, 2))
    numerator = jnp.abs(upper - 2.0 * center + lower) + jnp.abs(right - 2.0 * center + left)
    denominator = jnp.maximum(jnp.abs(upper) + 2.0 * jnp.abs(center) + jnp.abs(lower), 1.0)
    sensor[...] = jnp.swapaxes(numerator / denominator, 0, 1)


def shards(coefficients, mode_basis, shifts, owners):
    per_device = coefficients.shape[0]
    queries = owners.shape[0]
    frames, modes, rows, cells = mode_basis.shape
    bf16, f32 = jnp.bfloat16, jnp.float32
    block = (RING, RING, LANES)
    hbm = pl.BlockSpec(memory_space=pltpu.HBM)
    dma = pltpu.SemaphoreType.DMA
    field = pl.pallas_call(
        kernel,
        out_shape=jax.ShapeDtypeStruct((rows + 2, per_device, cells), bf16),
        in_specs=[hbm, hbm, hbm, hbm],
        out_specs=hbm,
        scratch_shapes=[
            pltpu.VMEM((rows, per_device, cells), bf16),
            pltpu.VMEM((2, per_device, cells), bf16),
            pltpu.SMEM((frames, queries), jnp.int32),
            pltpu.VMEM((1, queries), jnp.int32),
            pltpu.VMEM((frames, per_device, modes), bf16),
            pltpu.VMEM((frames, modes, rows, cells), bf16),
            pltpu.VMEM((frames, rows, modes, cells), bf16),
            pltpu.VMEM((RING, frames - 1, RING, LANES), bf16),
            pltpu.VMEM((RING, frames - 1, RING, LANES), bf16),
            pltpu.VMEM((RING, frames - 1, RING, LANES), bf16),
            pltpu.VMEM((RING, frames - 1, RING, LANES), bf16),
            pltpu.VMEM((RING, 1, RING, LANES), bf16),
            pltpu.VMEM((RING, 1, RING, LANES), bf16),
            pltpu.VMEM((RING, 1, RING, LANES), bf16),
            pltpu.VMEM((RING, 1, RING, LANES), bf16),
            pltpu.VMEM((PARTS, frames, 2, 256, LANES), f32),
            pltpu.VMEM(block, bf16),
            pltpu.VMEM((2 * RING, RING, LANES), bf16),
            pltpu.VMEM(block, bf16),
            pltpu.VMEM(block, bf16),
            pltpu.VMEM((RING, frames, RING, LANES), bf16),
            pltpu.VMEM((RING, frames, RING, LANES), bf16),
            pltpu.VMEM((RING, frames, RING, LANES), bf16),
            pltpu.VMEM((RING, frames, RING, LANES), bf16),
            pltpu.VMEM(block, bf16),
            pltpu.VMEM(block, bf16),
            pltpu.VMEM(block, bf16),
            pltpu.VMEM((2 * RING, RING, LANES), bf16),
            dma((frames,)), dma((3,)), dma(()),
            dma((3,)), dma((3,)), dma((3,)),
            dma((3,)), dma((3,)), dma((3,)),
            dma((PARTS,)), dma((PARTS,)), dma((PARTS,)),
            dma((PARTS,)), dma((PARTS,)), dma((PARTS,)),
            dma((2,)), dma((2,)),
        ],
        compiler_params=pltpu.CompilerParams(
            collective_id=0, has_side_effects=True, vmem_limit_bytes=63 * 1024 * 1024
        ),
    )(jnp.swapaxes(coefficients, 0, 1), mode_basis, shifts.T, owners.reshape(1, queries))
    part = 8
    out = pl.BlockSpec((part, rows, cells), lambda i: (i, 0, 0))
    recon, sensor = pl.pallas_call(
        finish,
        grid=(per_device // part,),
        out_shape=[jax.ShapeDtypeStruct((per_device, rows, cells), f32)] * 2,
        in_specs=[pl.BlockSpec((rows + 2, part, cells), lambda i: (0, i, 0))],
        out_specs=[out, out],
        compiler_params=pltpu.CompilerParams(vmem_limit_bytes=63 * 1024 * 1024),
    )(field)
    return recon, sensor


def solution(mesh):
    placed = (P("query", None, None), P(None, None, "loop", None), P(), P())
    return jax.shard_map(
        shards,
        mesh=mesh,
        in_specs=placed,
        out_specs=(P("query", "loop", None), P("query", "loop", None)),
        check_vma=False,
    )
```

```python
import functools

import jax
import jax.numpy as jnp
from jax import lax
from jax.experimental import pallas as pl
from jax.experimental.pallas import tpu as pltpu
from jax.sharding import PartitionSpec as P

MESH = pl.DeviceIdType.MESH
RING = 16
LANES = 128
WIDE = 4
PARTS = 2


def swapped(tiles, step=1, stop=2 * RING, blocks=2 * RING):
    lane = lax.broadcasted_iota(jnp.int32, tiles[0].shape, 1)
    count = len(tiles)
    while step < stop:
        width = step * (LANES // blocks)
        low = (lane // width) % 2 == 0
        new = [None] * count
        for i in range(count):
            if i & step:
                continue
            a, b = tiles[i], tiles[i | step]
            new[i] = jnp.where(low, a, pltpu.roll(b, width, 1))
            new[i | step] = jnp.where(low, pltpu.roll(a, LANES - width, 1), b)
        tiles = new
        step = step * 2
    return tiles


def kernel(
    coef, basis, shifts, owners, field,
    rows_in, edges, shift_in, owner_row, coefs, raw, modes, s1, r1, s2, r2, e1, f1, e2, f2, long, s3, r3, s4, r4,
    p1, q1, p2, q2, p3, q3, p4, q4,
    basis_sem, small_sem, field_sem, send1, recv1, own1, send2, recv2, own2,
    send3, recv3, own3, send4, recv4, own4, halo_send, halo_recv,
):
    me = lax.axis_index("loop")
    group = lax.axis_index("query")
    devices = lax.axis_size("loop")
    core = me % 2
    z = (me // 2) % RING
    sup = me // (2 * RING)
    spot = sup * 2 + core
    before = (me + devices - 1) % devices
    after = (me + 1) % devices

    def at_z(i):
        return sup * (2 * RING) + i * 2 + core

    def at_spot(i):
        return (i // 2) * (2 * RING) + z * 2 + i % 2

    plane = 2 * RING
    seat = group * RING + spot

    def in_plane(i):
        return {"loop": at_spot(i % RING), "query": i // RING}

    def farthest_first(k):
        return RING // 2 + (1 - 2 * (k % 2)) * ((k + 1) // 2)

    barrier = pltpu.get_barrier_semaphore()

    def greet_z(k, carry):
        i = (z + farthest_first(k)) % RING
        pl.semaphore_signal(barrier, inc=1, device_id={"loop": at_z(i)}, device_id_type=MESH)
        return carry

    def greet_plane(d, carry):
        pl.semaphore_signal(barrier, inc=1, device_id=in_plane((seat + d) % plane), device_id_type=MESH)
        return carry

    frames = basis.shape[0]
    depth = basis.shape[1] // 2
    loads = [
        pltpu.make_async_copy(basis.at[f, pl.ds(p * depth, depth)], raw.at[f, pl.ds(p * depth, depth)], basis_sem.at[f, p])
        for f in range(frames) for p in range(2)
    ]
    small = [
        pltpu.make_async_copy(coef, coefs, small_sem.at[0]),
        pltpu.make_async_copy(owners, owner_row, small_sem.at[1]),
        pltpu.make_async_copy(shifts, shift_in, small_sem.at[2]),
    ]
    loads[0].start()
    loads[1].start()
    small[0].start()
    lax.fori_loop(0, RING - 1, greet_z, 0, unroll=True)
    for load in loads[2:] + small[1:]:
        load.start()
    lax.fori_loop(1, plane, greet_plane, 0, unroll=True)
    pl.semaphore_signal(barrier, inc=1, device_id={"loop": before}, device_id_type=MESH)
    pl.semaphore_signal(barrier, inc=1, device_id={"loop": after}, device_id_type=MESH)

    def spread(source, target, here, to, send_sem, recv_sem, own_sem):
        pltpu.make_async_copy(source.at[here], target.at[here], own_sem).start()

        def one(k, carry):
            i = (here + farthest_first(k)) % RING
            pltpu.make_async_remote_copy(
                src_ref=source.at[i], dst_ref=target.at[here], send_sem=send_sem, recv_sem=recv_sem,
                device_id={"loop": to(i)}, device_id_type=MESH,
            ).start()
            return carry

        lax.fori_loop(0, RING - 1, one, 0, unroll=True)

    def landed(source, target, here, recv_sem, own_sem):
        pltpu.make_async_copy(source.at[here], target.at[here], own_sem).wait()
        most = target.at[pl.ds(0, RING - 1)]
        pltpu.make_async_copy(most, most, recv_sem).wait()

    def sent(source, send_sem):
        most = source.at[pl.ds(0, RING - 1)]
        pltpu.make_async_copy(most, most, send_sem).wait()

    def first(h, f):
        spread(s1.at[h, f], r1.at[h, f], z, at_z, send1.at[h, f], recv1.at[h, f], own1.at[h, f])

    def spread_plane(source, target, send_sem, recv_sem, own_sem):
        pltpu.make_async_copy(source.at[spot], target.at[seat], own_sem).start()

        def one(d, carry):
            i = (seat + d) % plane
            pltpu.make_async_remote_copy(
                src_ref=source.at[i % RING], dst_ref=target.at[seat], send_sem=send_sem, recv_sem=recv_sem,
                device_id=in_plane(i), device_id_type=MESH,
            ).start()
            return carry

        lax.fori_loop(1, plane, one, 0, unroll=True)

    def landed_plane(source, target, recv_sem, own_sem):
        pltpu.make_async_copy(source.at[spot], target.at[seat], own_sem).wait()
        most = target.at[pl.ds(0, plane - 1)]
        pltpu.make_async_copy(most, most, recv_sem).wait()

    def sent_plane(target, send_sem):
        most = target.at[pl.ds(0, plane - 1)]
        pltpu.make_async_copy(most, most, send_sem).wait()

    last = 2
    early = frames - 1
    trains = [(0, range(early), s1, r1, s2, r2), (1, range(early, frames), e1, f1, e2, f2)]
    for k, members, out, into, _, _ in trains:
        for f in members:
            loads[2 * f].wait()
            loads[2 * f + 1].wait()
            modes[f] = jnp.swapaxes(raw[f], 0, 1)
            if f == 0:
                small[0].wait()
            weights = coefs[f]
            tiles = [
                jnp.dot(weights, modes[f, x], preferred_element_type=jnp.float32).astype(jnp.bfloat16)
                for x in range(2 * RING)
            ]
            tiles = swapped(tiles)
            for i in range(RING):
                out[i, f - members[0]] = tiles[i]
            p1[:, f] = jnp.swapaxes(jnp.stack(tiles[RING:]), 0, 1)
        if k == 0:
            pl.semaphore_wait(barrier, RING - 1 + plane - 1 + 2)
        spread(out, into, z, at_z, send1.at[k], recv1.at[k], own1.at[k])
    spread(p1, q1, spot, at_spot, send2.at[last], recv2.at[last], own2.at[last])

    queries = owners.shape[1]
    small[1].wait()
    small[2].wait()
    mine = jnp.broadcast_to((owner_row[...] == group).astype(jnp.float32), (RING, queries))
    row = lax.broadcasted_iota(jnp.int32, (queries, queries), 0)
    column = lax.broadcasted_iota(jnp.int32, (queries, queries), 1)
    triangle = (row < column).astype(jnp.bfloat16)
    rank = jnp.dot(mine.astype(jnp.bfloat16), triangle, preferred_element_type=jnp.float32)
    slot = lax.broadcasted_iota(jnp.int32, (RING, queries), 0).astype(jnp.float32)
    picked = jnp.where(rank == slot, mine, 0.0).astype(jnp.bfloat16)
    cells_of = [shift_in[f, seat] for f in range(frames)]

    lane = lax.broadcasted_iota(jnp.int32, (128, LANES), 1)

    def store_long(h, f, i, part):
        part = part.astype(jnp.float32)
        at = (i // 2) * RING
        long[h, f, i % 2, at:at + RING] = part
        long[h, f, i % 2, 128 + at:128 + at + RING] = part

    def summed(h):
        sums = []
        for j in range(2):
            total = None
            for f in range(frames):
                rows = cells_of[f] // 32
                turn = (cells_of[f] % 32) * WIDE

                def moved(rows):
                    low = rows % 2
                    down = (rows // 2 + (j < low).astype(jnp.int32)) % 128
                    return long[h, f, (j + 2 - low) % 2, pl.ds(128 - down, 128), :]

                both = jnp.where(lane >= LANES - turn, moved(rows + 1), moved(rows))
                both = pltpu.roll(both, turn, 1)
                total = both if total is None else total + both
            sums.append(total.astype(jnp.bfloat16))
        return [sums[i % 2][(i // 2) * RING:(i // 2 + 1) * RING] for i in range(RING)]

    def owned(blocks):
        blocks = jnp.swapaxes(blocks, 0, 1)
        return [
            jnp.dot(picked, blocks[i], preferred_element_type=jnp.float32).astype(jnp.bfloat16)
            for i in range(RING)
        ]

    landed(p1, q1, spot, recv2.at[last], own2.at[last])
    for f in range(frames):
        p2[:, f] = jnp.swapaxes(q1[:, f], 0, 1)
    spread(p2, q2, z, at_z, send1.at[last], recv1.at[last], own1.at[last])

    for k, members, out, into, out2, _ in trains:
        landed(out, into, z, recv1.at[k], own1.at[k])
        for n in range(len(members)):
            out2[:, n] = jnp.swapaxes(into[:, n], 0, 1)
        spread(out2, trains[k][5], spot, at_spot, send2.at[k], recv2.at[k], own2.at[k])
    for k, members, _, _, out2, into2 in trains:
        landed(out2, into2, spot, recv2.at[k], own2.at[k])
        for f in members:
            for i in range(RING):
                store_long(0, f, i, into2[i, f - members[0]])
    parts = summed(0)
    for i in range(RING):
        s3[i] = parts[i]
    spread_plane(s3, r3, send3.at[0], recv3.at[0], own3.at[0])

    landed(p2, q2, z, recv1.at[last], own1.at[last])
    for f in range(frames):
        blocks = jnp.swapaxes(q2[:, f], 0, 1)
        for i in range(RING):
            store_long(1, f, i, blocks[i])
    p3[...] = jnp.swapaxes(jnp.stack(summed(1)), 0, 1)
    spread(p3, q3, z, at_z, send4.at[1], recv4.at[1], own4.at[1])

    landed_plane(s3, r3, recv3.at[0], own3.at[0])
    parts = owned(r3[...])
    for i in range(RING):
        s4[i] = parts[i]
    spread(s4, r4, z, at_z, send4.at[0], recv4.at[0], own4.at[0])

    landed(p3, q3, z, recv4.at[1], own4.at[1])
    p4[...] = jnp.swapaxes(q3[...], 0, 1)
    spread_plane(p4, q4, send3.at[1], recv3.at[1], own3.at[1])

    length = 2 * RING
    place = lax.broadcasted_iota(jnp.int32, (RING, LANES), 1) // WIDE

    def edge(row, tiles, block, x):
        for i, tile in enumerate(tiles):
            row = jnp.where(place == block + i, pltpu.roll(tile, (block + i - x) * WIDE % LANES, 1), row)
        return row

    blank = jnp.zeros((RING, LANES), jnp.bfloat16)
    landed(s4, r4, z, recv4.at[0], own4.at[0])
    early_tiles = [r4[i] for i in range(RING)]
    first_row = edge(blank, early_tiles, 0, 0)
    last_row = edge(blank, early_tiles, 0, length - 1)
    early_tiles = swapped(early_tiles, 1, RING)
    landed_plane(p4, q4, recv3.at[1], own3.at[1])
    late_tiles = owned(q4[...])
    edges[0] = edge(first_row, late_tiles, RING, 0)
    edges[1] = edge(last_row, late_tiles, RING, length - 1)
    up = pltpu.make_async_remote_copy(
        src_ref=edges.at[1], dst_ref=field.at[0], send_sem=halo_send.at[0], recv_sem=halo_recv.at[0],
        device_id={"loop": after}, device_id_type=MESH,
    )
    down = pltpu.make_async_remote_copy(
        src_ref=edges.at[0], dst_ref=field.at[length + 1], send_sem=halo_send.at[1], recv_sem=halo_recv.at[1],
        device_id={"loop": before}, device_id_type=MESH,
    )
    up.start()
    down.start()
    tiles = swapped(early_tiles + swapped(late_tiles, 1, RING), RING, length)
    for x in range(length):
        rows_in[x] = tiles[x]
    inside = pltpu.make_async_copy(rows_in, field.at[pl.ds(1, length)], field_sem)
    inside.start()
    for k, _, out, _, out2, _ in trains:
        sent(out, send1.at[k])
        sent(out2, send2.at[k])
    sent(p1, send2.at[last])
    sent(p2, send1.at[last])
    sent_plane(r3, send3.at[0])
    sent(s4, send4.at[0])
    sent(p3, send4.at[1])
    sent_plane(q4, send3.at[1])
    inside.wait()
    up.wait()
    down.wait()


def finish(field, recon, sensor):
    u = field[...].astype(jnp.float32)
    center, upper, lower = u[1:-1], u[2:], u[:-2]
    recon[...] = jnp.swapaxes(center, 0, 1)
    place = lax.broadcasted_iota(jnp.int32, center.shape, 2)
    right = jnp.where(place == LANES - 1, 0.0, pltpu.roll(center, LANES - 1, 2))
    left = jnp.where(place == 0, 0.0, pltpu.roll(center, 1, 2))
    numerator = jnp.abs(upper - 2.0 * center + lower) + jnp.abs(right - 2.0 * center + left)
    denominator = jnp.maximum(jnp.abs(upper) + 2.0 * jnp.abs(center) + jnp.abs(lower), 1.0)
    sensor[...] = jnp.swapaxes(numerator / denominator, 0, 1)


def shards(coefficients, mode_basis, shifts, owners):
    per_device = coefficients.shape[0]
    queries = owners.shape[0]
    frames, modes, rows, cells = mode_basis.shape
    bf16, f32 = jnp.bfloat16, jnp.float32
    block = (RING, RING, LANES)
    hbm = pl.BlockSpec(memory_space=pltpu.HBM)
    dma = pltpu.SemaphoreType.DMA
    field = pl.pallas_call(
        kernel,
        out_shape=jax.ShapeDtypeStruct((rows + 2, per_device, cells), bf16),
        in_specs=[hbm, hbm, hbm, hbm],
        out_specs=hbm,
        scratch_shapes=[
            pltpu.VMEM((rows, per_device, cells), bf16),
            pltpu.VMEM((2, per_device, cells), bf16),
            pltpu.SMEM((frames, queries), jnp.int32),
            pltpu.VMEM((1, queries), jnp.int32),
            pltpu.VMEM((frames, per_device, modes), bf16),
            pltpu.VMEM((frames, modes, rows, cells), bf16),
            pltpu.VMEM((frames, rows, modes, cells), bf16),
            pltpu.VMEM((RING, frames - 1, RING, LANES), bf16),
            pltpu.VMEM((RING, frames - 1, RING, LANES), bf16),
            pltpu.VMEM((RING, frames - 1, RING, LANES), bf16),
            pltpu.VMEM((RING, frames - 1, RING, LANES), bf16),
            pltpu.VMEM((RING, 1, RING, LANES), bf16),
            pltpu.VMEM((RING, 1, RING, LANES), bf16),
            pltpu.VMEM((RING, 1, RING, LANES), bf16),
            pltpu.VMEM((RING, 1, RING, LANES), bf16),
            pltpu.VMEM((PARTS, frames, 2, 256, LANES), f32),
            pltpu.VMEM(block, bf16),
            pltpu.VMEM((2 * RING, RING, LANES), bf16),
            pltpu.VMEM(block, bf16),
            pltpu.VMEM(block, bf16),
            pltpu.VMEM((RING, frames, RING, LANES), bf16),
            pltpu.VMEM((RING, frames, RING, LANES), bf16),
            pltpu.VMEM((RING, frames, RING, LANES), bf16),
            pltpu.VMEM((RING, frames, RING, LANES), bf16),
            pltpu.VMEM(block, bf16),
            pltpu.VMEM(block, bf16),
            pltpu.VMEM(block, bf16),
            pltpu.VMEM((2 * RING, RING, LANES), bf16),
            dma((frames, 2)), dma((3,)), dma(()),
            dma((3,)), dma((3,)), dma((3,)),
            dma((3,)), dma((3,)), dma((3,)),
            dma((PARTS,)), dma((PARTS,)), dma((PARTS,)),
            dma((PARTS,)), dma((PARTS,)), dma((PARTS,)),
            dma((2,)), dma((2,)),
        ],
        compiler_params=pltpu.CompilerParams(
            collective_id=0, has_side_effects=True, vmem_limit_bytes=63 * 1024 * 1024
        ),
    )(jnp.swapaxes(coefficients, 0, 1), mode_basis, shifts.T, owners.reshape(1, queries))
    part = 8
    out = pl.BlockSpec((part, rows, cells), lambda i: (i, 0, 0))
    recon, sensor = pl.pallas_call(
        finish,
        grid=(per_device // part,),
        out_shape=[jax.ShapeDtypeStruct((per_device, rows, cells), f32)] * 2,
        in_specs=[pl.BlockSpec((rows + 2, part, cells), lambda i: (0, i, 0))],
        out_specs=[out, out],
        compiler_params=pltpu.CompilerParams(vmem_limit_bytes=63 * 1024 * 1024),
    )(field)
    return recon, sensor


def solution(mesh):
    placed = (P("query", None, None), P(None, None, "loop", None), P(), P())
    return jax.shard_map(
        shards,
        mesh=mesh,
        in_specs=placed,
        out_specs=(P("query", "loop", None), P("query", "loop", None)),
        check_vma=False,
    )
```
